256 devices in a mesh: dp: 8 (over x, core), expert: 32 (over z, y).
Axes of the slice: x: 4, y: 4, z: 8, core: 2. Of those that a mesh axis runs over, the one named last changes fastest.
Arguments:
- x_rows: bfloat16 [8, 32, 256, 4096], P('dp', 'expert'), may hold values from -6 to 6
- out_grads: bfloat16 [8, 32, 256, 3072], P('dp', 'expert'), may hold values from -6 to 6
- token_counts: int32 [8, 32], P(None, 'expert'), may hold values from 1 to 256, as said below
- a_param: float32 [32, 4096, 128], P('expert', 'dp'), may hold values from -1.5 to 1.5
- a_first: float32 [32, 4096, 128], P('expert', 'dp'), may hold values from -1.8 to 1.8
- a_second: float32 [32, 4096, 128], P('expert', 'dp'), may hold values from 0.01 to 1
- b_param: float32 [32, 64, 3072], P('expert', None, 'dp'), may hold values from -1.5 to 1.5
- b_first: float32 [32, 64, 3072], P('expert', None, 'dp'), may hold values from -1.8 to 1.8
- b_second: float32 [32, 64, 3072], P('expert', None, 'dp'), may hold values from 0.01 to 1
- frozen_tiles: bfloat16 [32, 4096, 3072], P('expert', 'dp'), may hold values from -6 to 6
- placement_map: int32 [512], replicated, may hold values from 0 to 1023, as said below
Outputs:
- new_a: float32 [32, 4096, 128], P('expert', 'dp')
- new_a_first: float32 [32, 4096, 128], P('expert', 'dp')
- new_a_second: float32 [32, 4096, 128], P('expert', 'dp')
- new_b: float32 [32, 64, 3072], P('expert', None, 'dp')
- new_b_first: float32 [32, 64, 3072], P('expert', None, 'dp')
- new_b_second: float32 [32, 64, 3072], P('expert', None, 'dp')
- served: bfloat16 [512, 8, 16, 3072], P('expert', 'dp')
The draws below stay inside these ranges and needn't reach their ends.
Inputs may be any that keep to these rules, and one draw needn't show every extreme that they name: `token_counts`: at least 1; the largest entry equals 256 in every draw. `placement_map`: server slot s belongs to the server owner s // 16 of the expert axis. Each owner takes exactly one tile from each of 16 distinct trainer devices (the trainer device of tile t is t // 32), and none from the others; how often a tile is hosted varies.
All inputs are finite; a program needn't handle non-finite values.
Results may differ from the reference program's by a relative error of at most 0.005.
Values may be sent and summed in bfloat16 or wider, within the bound.
No kernel may reach another device: no remote copies, remote signals or barrier semaphores. Data moves between devices by JAX's collectives and lax.ppermute only.
A program may use at most 128 MiB of HBM per device.

```python
import math
import jax
import jax.numpy as jnp
from jax import lax

D = 4096
EXPERT_HIDDEN = 1536
LOW_RANK = 64
EXP_DEV = 1
CAP = 256
TILE_ROWS = 16
PAIR_MOST = 1
SLOTS = 16
EXPERTS = 32
TPD = 32
SERVER_SLOTS = 512
N_DP = 8


def draw_token_counts(key, part):
    key = jax.random.fold_in(key, 5)
    key_hot, key_raw, key_pick = jax.random.split(key, 3)
    hotness = jax.random.randint(key_hot, (EXPERTS,), 1, 9)
    raw_counts = jax.random.randint(key_raw, (N_DP, EXPERTS), 1, CAP + 1)
    counts = jnp.maximum(1, raw_counts * hotness[None, :] // 8)
    chosen = jax.random.randint(key_pick, (), 0, EXPERTS)
    full_row = (jnp.arange(N_DP)[:, None] == 0) & (jnp.arange(EXPERTS)[None, :] == chosen)
    return jnp.where(full_row, CAP, counts).astype(jnp.int32)


def draw_placement_map(key, part):
    key = jax.random.fold_in(key, 7)
    key_hot, key_score, key_start, key_order = jax.random.split(key, 4)
    owners = SERVER_SLOTS // SLOTS
    sources = SLOTS // PAIR_MOST
    local_tiles = EXP_DEV * TPD
    hotness = jax.random.randint(key_hot, (owners,), 0, 4)
    scores = hotness[None, :] * (4 * owners) + jax.random.randint(key_score, (owners, owners), 0, 4 * owners)
    scores = scores * owners + jnp.arange(owners)[None, :]
    owner_grid = jnp.arange(owners)[:, None]
    device_grid = jnp.arange(owners)[None, :]
    forced = (owner_grid == 0) & (device_grid == owners - 1) | (owner_grid == owners - 1) & (device_grid == 0)
    scores = scores + jnp.where(forced, 64 * owners * owners, 0)
    unused, chosen = lax.top_k(scores, sources)
    start = jax.random.randint(key_start, (owners, sources), 0, local_tiles)
    owner_rows = jnp.arange(owners)[:, None]
    start = jnp.where((owner_rows == 0) & (chosen == owners - 1), local_tiles - PAIR_MOST, start)
    start = jnp.where((owner_rows == owners - 1) & (chosen == 0), 0, start)
    within = (start[:, :, None] + jnp.arange(PAIR_MOST)[None, None, :]) % local_tiles
    ids = (chosen[:, :, None] * local_tiles + within).reshape(owners, SLOTS)
    shuffle = jax.random.randint(key_order, (owners, SLOTS), 0, 4 * SLOTS) * SLOTS + jnp.arange(SLOTS)[None, :]
    ordering = jnp.argsort(shuffle, axis=1)
    ids = jnp.take_along_axis(ids, ordering, axis=1)
    return ids.reshape(-1).astype(jnp.int32)


def block_scale(key, shape, cuts, smallest, top_value):
    gain, own = 1.0, jax.random.fold_in(key, 6)
    for dim, blocks in cuts:
        heights = jnp.exp(jax.random.uniform(jax.random.fold_in(own, dim), (blocks,), jnp.float32, smallest / len(cuts), top_value / len(cuts)))
        gain = gain * jnp.repeat(heights, shape[dim] // blocks).reshape([-1 if axis == dim else 1 for axis in range(len(shape))])
    return gain


def gaussian(stream_key, shape, scale, most, shards=(), dtype=jnp.bfloat16):
    level = block_scale(stream_key, shape, shards, -0.22, 0.18) if shards else 1.0
    array = jax.random.normal(stream_key, shape, jnp.float32) * scale * level
    return jnp.minimum(jnp.maximum(array, -most), most).astype(dtype)


def setup_inputs(seed: int = 0) -> dict:
    arg_keys = jax.random.split(jax.random.key(seed), 12)
    x_rows = gaussian(arg_keys[0], (N_DP, EXPERTS, CAP, D), 1.0, 6.0, ((0, 8), (1, 32)))
    out_grads = gaussian(arg_keys[1], (N_DP, EXPERTS, CAP, 2 * EXPERT_HIDDEN), 1.0, 6.0, ((0, 8), (1, 32)))
    token_counts = draw_token_counts(jax.random.fold_in(arg_keys[11], 71), 0)
    a_param = gaussian(arg_keys[3], (EXPERTS, D, 2 * LOW_RANK), 0.25, 1.5, ((0, 32), (1, 8)), jnp.float32)
    a_first = gaussian(arg_keys[4], (EXPERTS, D, 2 * LOW_RANK), 0.3, 1.8, ((0, 32), (1, 8)), jnp.float32)
    a_second = jnp.clip(jnp.exp(math.log(1.0) - 4.6051702 * jax.random.uniform(arg_keys[5], (EXPERTS, D, 2 * LOW_RANK), jnp.float32) ** block_scale(arg_keys[5], (EXPERTS, D, 2 * LOW_RANK), ((0, 32), (1, 8)), -0.2, 0.2)), 0.01, 1.0)
    b_param = gaussian(arg_keys[6], (EXPERTS, LOW_RANK, 2 * EXPERT_HIDDEN), 0.25, 1.5, ((0, 32), (2, 8)), jnp.float32)
    b_first = gaussian(arg_keys[7], (EXPERTS, LOW_RANK, 2 * EXPERT_HIDDEN), 0.3, 1.8, ((0, 32), (2, 8)), jnp.float32)
    b_second = jnp.clip(jnp.exp(math.log(1.0) - 4.6051702 * jax.random.uniform(arg_keys[8], (EXPERTS, LOW_RANK, 2 * EXPERT_HIDDEN), jnp.float32) ** block_scale(arg_keys[8], (EXPERTS, LOW_RANK, 2 * EXPERT_HIDDEN), ((0, 32), (2, 8)), -0.2, 0.2)), 0.01, 1.0)
    frozen_tiles = gaussian(arg_keys[9], (EXPERTS, D, 2 * EXPERT_HIDDEN), 1.0, 6.0, ((0, 32), (1, 8)))
    placement_map = draw_placement_map(jax.random.fold_in(arg_keys[11], 71), 0)
    return {"x_rows": x_rows, "out_grads": out_grads, "token_counts": token_counts, "a_param": a_param, "a_first": a_first, "a_second": a_second, "b_param": b_param, "b_first": b_first, "b_second": b_second, "frozen_tiles": frozen_tiles, "placement_map": placement_map}


beta_one = 0.9
beta_two = 0.95
learn_rate = 0.05
adam_eps = 1e-08
bias_one = 1.0 - 0.9 ** 10
bias_two = 1.0 - 0.95 ** 10
adapter_scale = 2.0

def adam_step(weights, moment_one, moment_two, gradient):
    moment_one = beta_one * moment_one + (1.0 - beta_one) * gradient
    moment_two = beta_two * moment_two + (1.0 - beta_two) * gradient * gradient
    update_step = learn_rate * (moment_one / bias_one) / (jnp.sqrt(moment_two / bias_two) + adam_eps)
    return (weights - update_step, moment_one, moment_two)

def reference(x_rows, out_grads, token_counts, a_param, a_first, a_second, b_param, b_first, b_second, frozen_tiles, placement_map):
    single_precision = jnp.float32
    total_tokens = lax.optimization_barrier(jnp.sum(token_counts, axis=0)).astype(single_precision)
    a_half = a_param.astype(jnp.bfloat16)
    b_half = b_param.astype(jnp.bfloat16)

    def expert_grads(expert_number):
        input_rows = x_rows[:, expert_number].astype(single_precision)
        out_rows = out_grads[:, expert_number]
        live_rows = token_counts[:, expert_number]
        row_mask = jnp.arange(CAP)[None, :] < live_rows[:, None]
        active_gradients = jnp.where(row_mask[:, :, None], out_rows, jnp.zeros((), jnp.bfloat16)).astype(single_precision)
        a_expert = a_half[expert_number].astype(single_precision)
        b_expert = b_half[expert_number].astype(single_precision)
        projected_rows = jnp.einsum('pcd,dk->pck', input_rows, a_expert).astype(jnp.bfloat16).astype(single_precision)
        reverse_pass = jnp.concatenate([jnp.einsum('pcf,kf->pck', active_gradients[:, :, :EXPERT_HIDDEN], b_expert[:, :EXPERT_HIDDEN]), jnp.einsum('pcf,kf->pck', active_gradients[:, :, EXPERT_HIDDEN:], b_expert[:, EXPERT_HIDDEN:])], axis=2)
        reverse_pass = reverse_pass.astype(jnp.bfloat16).astype(single_precision)
        down_factor_gradient = adapter_scale * jnp.einsum('zxq,zxl->ql', input_rows, reverse_pass)
        up_factor_gradient = adapter_scale * jnp.concatenate([jnp.einsum('esj,esb->jb', projected_rows[:, :, :LOW_RANK], active_gradients[:, :, :EXPERT_HIDDEN]), jnp.einsum('esj,esb->jb', projected_rows[:, :, LOW_RANK:], active_gradients[:, :, EXPERT_HIDDEN:])], axis=1)
        return (down_factor_gradient / total_tokens[expert_number], up_factor_gradient / total_tokens[expert_number])
    down_factor_gradient, up_factor_gradient = lax.map(expert_grads, jnp.arange(EXPERTS))
    new_a, new_a_first, new_a_second = adam_step(a_param, a_first, a_second, down_factor_gradient)
    new_b, new_b_first, new_b_second = adam_step(b_param, b_first, b_second, up_factor_gradient)
    a_new_half = new_a.astype(jnp.bfloat16)
    b_new_half = new_b.astype(jnp.bfloat16)

    def merge_one(expert_number):
        a_expert = a_new_half[expert_number].astype(single_precision)
        b_expert = b_new_half[expert_number].astype(single_precision)
        weight_change = jnp.concatenate([jnp.einsum('dk,kf->df', a_expert[:, :LOW_RANK], b_expert[:, :EXPERT_HIDDEN]), jnp.einsum('dk,kf->df', a_expert[:, LOW_RANK:], b_expert[:, EXPERT_HIDDEN:])], axis=1)
        return (frozen_tiles[expert_number].astype(single_precision) + adapter_scale * weight_change).astype(jnp.bfloat16)
    merged = lax.map(merge_one, jnp.arange(EXPERTS))
    tile_grid = merged.reshape(EXPERTS, N_DP, TPD, TILE_ROWS, 2 * EXPERT_HIDDEN)
    expert_id = (placement_map // TPD).astype(jnp.int32)
    tile_index = (placement_map % TPD).astype(jnp.int32)
    served = tile_grid[expert_id, :, tile_index]
    return (new_a, new_a_first, new_a_second, new_b, new_b_first, new_b_second, served)
```

```python
import functools

import jax
import jax.numpy as jnp
from jax import lax
from jax.experimental import pallas as pl
from jax.experimental.pallas import tpu as pltpu
from jax.sharding import PartitionSpec as P

LOW_RANK = 64
TILE_ROWS = 16
TILES = 32
SLOTS = 16
Z, Y, DP = 8, 4, 8
X = 4

beta_one = 0.9
beta_two = 0.95
learn_rate = 0.05
adam_eps = 1e-08
bias_one = 1.0 - 0.9**10
bias_two = 1.0 - 0.95**10
adapter_scale = 2.0

F32 = jnp.float32
BF16 = jnp.bfloat16


def adam_step(weights, moment_one, moment_two, gradient):
    moment_one = beta_one * moment_one + (1.0 - beta_one) * gradient
    moment_two = beta_two * moment_two + (1.0 - beta_two) * gradient * gradient
    update_step = (
        learn_rate * (moment_one / bias_one) / (jnp.sqrt(moment_two / bias_two) + adam_eps)
    )
    return (weights - update_step, moment_one, moment_two)


def shift_x(array, k):
    return lax.ppermute(
        array, "dp", [(i, (i // 2 + k) % X * 2 + i % 2) for i in range(DP)]
    )


def swap_core(array):
    return lax.ppermute(array, "dp", [(i, i // 2 * 2 + 1 - i % 2) for i in range(DP)])


def shift_y(array, k):
    return lax.ppermute(
        array, "expert", [(i, i // Y * Y + (i % Y + k) % Y) for i in range(Z * Y)]
    )


def shift_z(array, k):
    return lax.ppermute(
        array, "expert", [(i, (i // Y + k) % Z * Y + i % Y) for i in range(Z * Y)]
    )


def vmem():
    return pl.BlockSpec(memory_space=pltpu.VMEM)


def smem():
    return pl.BlockSpec(memory_space=pltpu.SMEM)


def anywhere():
    return pl.BlockSpec(memory_space=pl.ANY)


PARAMS = pltpu.CompilerParams(vmem_limit_bytes=60 * 1024 * 1024)


def gradient_kernel(ids, counts, x, g, *refs):
    blocks, keep, give = refs[:DP], refs[DP], refs[DP + 1]
    chip, core = ids[0] // 2, lax.rem(ids[0], 2)
    live = counts[ids[0], 0]
    rows = x.shape[0]
    a_rows = x.shape[1] // DP
    cols = g.shape[1] // DP
    tiles = cols // 128
    projected = jnp.zeros((rows, 2 * LOW_RANK), F32)
    gate = jnp.zeros((rows, LOW_RANK), F32)
    up = jnp.zeros((rows, LOW_RANK), F32)
    for i in range(DP):
        k, c = i // 2, i % 2
        j = 2 * lax.rem(chip + X - k, X) + (1 - core if c else core)
        part = x[:, pl.ds(pl.multiple_of(j * a_rows, a_rows), a_rows)]
        projected += jnp.dot(part, blocks[i][:a_rows, :], preferred_element_type=F32)
        b_block = jnp.concatenate(
            [
                blocks[i][a_rows + t * LOW_RANK : a_rows + (t + 1) * LOW_RANK, :]
                for t in range(tiles)
            ],
            axis=1,
        )
        part = g[:, pl.ds(pl.multiple_of(j * cols, 128), cols)]
        term = lax.dot_general(
            part, b_block, (((1,), (1,)), ((), ())), preferred_element_type=F32
        )
        is_gate = j < DP // 2
        gate += jnp.where(is_gate, term, 0.0)
        up += jnp.where(is_gate, 0.0, term)
    mask = lax.broadcasted_iota(jnp.int32, (rows, 2 * LOW_RANK), 0) < live
    backward = jnp.where(mask, jnp.concatenate([gate, up], axis=1), 0.0)
    backward_t = jnp.transpose(backward).astype(BF16)
    projected_t = jnp.transpose(jnp.where(mask, projected, 0.0)).astype(BF16)
    for i in range(DP):
        k, c = i // 2, i % 2
        j = 2 * lax.rem(chip + k, X) + (1 - core if c else core)
        out = give if c else keep
        part = x[:, pl.ds(pl.multiple_of(j * a_rows, a_rows), a_rows)]
        grad = jnp.dot(backward_t, part, preferred_element_type=F32).astype(BF16)
        for t in range(a_rows // 128):
            out[k, t * 128 : (t + 1) * 128, :] = grad[:, t * 128 : (t + 1) * 128]
        part = g[:, pl.ds(pl.multiple_of(j * cols, 128), cols)]
        half = jnp.where(j < DP // 2, projected_t[:LOW_RANK], projected_t[LOW_RANK:])
        grad = jnp.dot(half, part, preferred_element_type=F32).astype(BF16)
        for t in range(tiles):
            out[k, a_rows + t * LOW_RANK : a_rows + (t + 1) * LOW_RANK, :] = grad[
                :, t * 128 : (t + 1) * 128
            ]


def pack_kernel(a, b, out):
    a_rows = a.shape[0]
    out[:a_rows, :] = a[...].astype(BF16)
    for t in range(b.shape[1] // 128):
        r = slice(a_rows + t * LOW_RANK, a_rows + (t + 1) * LOW_RANK)
        out[r, :] = b[:, t * 128 : (t + 1) * 128].astype(BF16)


def pair_kernel(kept, taken, *outs):
    for k in range(X):
        outs[k][...] = (kept[k].astype(F32) + taken[k].astype(F32)).astype(BF16)


def adam_kernel(ids, pick, counts, *refs):
    blocks = refs[:X]
    a, a1, a2, b, b1, b2 = refs[X : X + 6]
    na, na1, na2, nb, nb1, nb2 = refs[X + 6 : X + 12]
    outs, ah = refs[X + 12 : -1], refs[-1]
    tokens = counts[0, 0]
    for p in range(1, DP):
        tokens += counts[p, 0]
    factor = adapter_scale / jnp.full((1, 128), tokens, jnp.int32).astype(F32)
    a_rows = a.shape[0]
    b_rows = b.shape[1] // 128 * LOW_RANK

    def total(lo, hi):
        s = blocks[0][lo:hi, :].astype(F32)
        for k in range(1, X):
            s += blocks[k][lo:hi, :].astype(F32)
        return s * factor

    for t in range(b.shape[1] // 128):
        c = slice(t * 128, (t + 1) * 128)
        grad = total(a_rows + t * LOW_RANK, a_rows + (t + 1) * LOW_RANK)
        new, one, two = adam_step(b[:, c], b1[:, c], b2[:, c], grad)
        nb[:, c], nb1[:, c], nb2[:, c] = new, one, two
        for dz in range(Z):
            outs[dz][t * LOW_RANK : (t + 1) * LOW_RANK, :] = new.astype(BF16)
    for t in range(a_rows // 128):
        r = slice(t * 128, (t + 1) * 128)
        grad = jnp.transpose(total(t * 128, (t + 1) * 128))
        new, one, two = adam_step(a[r, :], a1[r, :], a2[r, :], grad)
        na[r, :], na1[r, :], na2[r, :] = new, one, two
        ah[r, :] = new.astype(BF16)
    z, y = ids[1] // Y, lax.rem(ids[1], Y)
    for dz in range(Z):
        for dy in range(Y):
            owner = lax.rem(z + dz, Z) * Y + lax.rem(y + dy, Y)
            start = pl.multiple_of(pick[owner] * TILE_ROWS, TILE_ROWS)
            r = slice(b_rows + dy * TILE_ROWS, b_rows + (dy + 1) * TILE_ROWS)
            outs[dz][r, :] = ah[pl.ds(start, TILE_ROWS), :]


def tiles_kernel(half, pick, frozen, out, sem):
    cols = out.shape[2]
    copies = []
    for owner in range(out.shape[0]):
        start = pl.multiple_of(pick[owner] * TILE_ROWS, TILE_ROWS)
        src = frozen.at[pl.ds(start, TILE_ROWS), pl.ds(half * cols, cols)]
        copies.append(pltpu.make_async_copy(src, out.at[owner], sem.at[owner]))
    for copy in copies:
        copy.start()
    for copy in copies:
        copy.wait()


def send_tiles(half, pick, frozen):
    shape = (Z * Y, TILE_ROWS, frozen.shape[1] // 2)
    return pl.pallas_call(
        functools.partial(tiles_kernel, half),
        out_shape=jax.ShapeDtypeStruct(shape, BF16),
        in_specs=[smem(), anywhere()],
        out_specs=vmem(),
        scratch_shapes=[pltpu.SemaphoreType.DMA((Z * Y,))],
        compiler_params=PARAMS,
        name="tiles",
    )(pick, frozen)


def stack_kernel(*refs):
    ins, up, downs = refs[:Z], refs[Z], refs[Z + 1 :]
    b_rows = up.shape[1]
    for i, ref in enumerate(ins):
        up[i] = ref[:b_rows, :]
        for dy, down in enumerate(downs):
            down[i] = ref[b_rows + dy * TILE_ROWS : b_rows + (dy + 1) * TILE_ROWS, :]


def slot_of(ids, table, s):
    source = table[ids[1] * SLOTS + s] // TILES
    dz = lax.rem(ids[1] // Y + Z - source // Y, Z)
    dy = lax.rem(lax.rem(ids[1], Y) + Y - lax.rem(source, Y), Y)
    return source, dz, dy


def delta_kernel(ids, table, *refs):
    ups, others, downs = refs[:Y], refs[Y : 2 * Y], refs[2 * Y : 2 * Y + X]
    outs, (own, other, sem) = refs[2 * Y + X : 2 * Y + 2 * X], refs[2 * Y + 2 * X :]
    n_tiles = own.shape[1] // LOW_RANK
    cols = n_tiles * 128
    chip, core = ids[0] // 2, lax.rem(ids[0], 2)
    places = []
    for s in range(SLOTS):
        _, dz, dy = slot_of(ids, table, s)
        places.append((dy, dz))
        for i in range(Y):

            @pl.when(dy == i)
            def _(s=s, i=i, dz=dz):
                pltpu.make_async_copy(ups[i].at[dz], own.at[s], sem.at[0, s]).start()
                pltpu.make_async_copy(others[i].at[dz], other.at[s], sem.at[1, s]).start()

    is_gate = chip < X // 2
    first = jnp.int32(0) == core
    for s in range(SLOTS):
        pltpu.make_async_copy(ups[0].at[0], own.at[s], sem.at[0, s]).wait()
        pltpu.make_async_copy(others[0].at[0], other.at[s], sem.at[1, s]).wait()
        left = jnp.concatenate([downs[k][places[s]] for k in range(X)], axis=0)
        left = jnp.where(is_gate, left[:, :LOW_RANK], left[:, LOW_RANK:])
        halves = []
        for ref in (own, other):
            right = jnp.concatenate(
                [ref[s, t * LOW_RANK : (t + 1) * LOW_RANK, :] for t in range(n_tiles)], axis=1
            )
            delta = adapter_scale * jnp.dot(left, right, preferred_element_type=F32)
            halves.append(delta.astype(BF16))
        mine, theirs = halves
        for k in range(X):
            r = slice(k * TILE_ROWS, (k + 1) * TILE_ROWS)
            outs[k][s, :, :cols] = jnp.where(first, mine[r], theirs[r])
            outs[k][s, :, cols:] = jnp.where(first, theirs[r], mine[r])


def merge_kernel(ids, table, low, high, *refs):
    deltas, out = refs[:X], refs[X]
    chip = ids[0] // 2
    cols = deltas[0].shape[2]
    width = low.shape[2]
    for s in range(SLOTS):
        source = table[ids[1] * SLOTS + s] // TILES
        out[s, :, :width] = low[source]
        out[s, :, width:] = high[source]
        for k in range(X):
            j = lax.rem(chip + k, X)
            c = pl.ds(pl.multiple_of(j * cols, 128), cols)
            out[s, :, c] = (out[s, :, c].astype(F32) + deltas[k][s].astype(F32)).astype(BF16)


def per_device(
    x_rows,
    out_grads,
    token_counts,
    a_param,
    a_first,
    a_second,
    b_param,
    b_first,
    b_second,
    frozen_tiles,
    placement_map,
):
    dp, expert = lax.axis_index("dp"), lax.axis_index("expert")
    ids = jnp.stack([dp, expert]).astype(jnp.int32)
    x, g = x_rows[0, 0], out_grads[0, 0]
    a, a1, a2 = a_param[0], a_first[0], a_second[0]
    b, b1, b2 = b_param[0], b_first[0], b_second[0]
    frozen = frozen_tiles[0]
    a_rows, width = a.shape[0], frozen.shape[1]
    cols = b.shape[1]
    shape_a, shape_b = jax.ShapeDtypeStruct(a.shape, F32), jax.ShapeDtypeStruct(b.shape, F32)
    shape_block = jax.ShapeDtypeStruct((a_rows + cols // 128 * LOW_RANK, 128), BF16)

    block = pl.pallas_call(
        pack_kernel,
        out_shape=shape_block,
        in_specs=[vmem()] * 2,
        out_specs=vmem(),
        compiler_params=PARAMS,
        name="pack",
    )(a, b)
    blocks = []
    for k in range(X):
        mine = block if k == 0 else shift_x(block, k)
        blocks += [mine, swap_core(mine)]

    table = placement_map.reshape(Z * Y, SLOTS)
    pick = jnp.sum(jnp.where(table // TILES == expert, table % TILES, 0), axis=1)
    low = lax.all_to_all(
        send_tiles(0, pick, frozen), "expert", split_axis=0, concat_axis=0, tiled=True
    )

    def update(x, g, a, a1, a2, b, b1, b2, ids, pick, *blocks):
        kept, given = pl.pallas_call(
            gradient_kernel,
            out_shape=[jax.ShapeDtypeStruct((X,) + shape_block.shape, BF16)] * 2,
            in_specs=[smem()] * 2 + [vmem()] * (2 + DP),
            out_specs=[vmem()] * 2,
            compiler_params=PARAMS,
            name="gradients",
        )(ids, token_counts, x, g, *blocks)
        taken = swap_core(given)
        pairs = pl.pallas_call(
            pair_kernel,
            out_shape=[shape_block] * X,
            in_specs=[vmem()] * 2,
            out_specs=[vmem()] * X,
            compiler_params=PARAMS,
            name="pairs",
        )(kept, taken)
        sums = [pairs[0]] + [shift_x(pairs[k], k) for k in range(1, X)]

        new_a, new_a1, new_a2, new_b, new_b1, new_b2, *messages = pl.pallas_call(
            adam_kernel,
            out_shape=[shape_a] * 3 + [shape_b] * 3 + [message] * Z,
            in_specs=[smem()] * 3 + [vmem()] * (X + 6),
            out_specs=[vmem()] * (6 + Z),
            scratch_shapes=[pltpu.VMEM(a.shape, BF16)],
            compiler_params=PARAMS,
            name="adam",
        )(ids, pick, token_counts, *sums, a, a1, a2, b, b1, b2)
        arrived = [messages[dz] if dz == 0 else shift_z(messages[dz], dz) for dz in range(Z)]
        return (new_a, new_a1, new_a2, new_b, new_b1, new_b2, *arrived)

    some = jnp.min(token_counts) > 0
    b_rows = cols // 128 * LOW_RANK
    message = jax.ShapeDtypeStruct((b_rows + Y * TILE_ROWS, 128), BF16)
    part = jax.ShapeDtypeStruct((SLOTS, TILE_ROWS, 2 * cols), BF16)

    def zeros(shapes):
        return lambda *_: tuple(jnp.zeros(s.shape, s.dtype) for s in shapes)

    outs = lax.cond(
        some,
        update,
        zeros([shape_a] * 3 + [shape_b] * 3 + [message] * Z),
        *(x, g, a, a1, a2, b, b1, b2, ids, pick, *blocks),
    )
    new_a, new_a1, new_a2, new_b, new_b1, new_b2 = outs[:6]

    high_out, low, arrived = lax.optimization_barrier(
        (send_tiles(1, pick, frozen), low, outs[6:])
    )
    high = lax.all_to_all(high_out, "expert", split_axis=0, concat_axis=0, tiled=True)

    def spread(ids, placement_map, *arrived):
        up, *downs = pl.pallas_call(
            stack_kernel,
            out_shape=[jax.ShapeDtypeStruct((Z, b_rows, 128), BF16)]
            + [jax.ShapeDtypeStruct((Z, TILE_ROWS, 128), BF16)] * Y,
            in_specs=[vmem()] * Z,
            out_specs=[vmem()] * (1 + Y),
            compiler_params=PARAMS,
            name="stack",
        )(*arrived)
        rows = jnp.stack([downs[0]] + [shift_y(downs[dy], dy) for dy in range(1, Y)])
        ups = [up] + [shift_y(up, dy) for dy in range(1, Y)]
        others = [swap_core(u) for u in ups]
        chips = [rows] + [shift_x(rows, k) for k in range(1, X)]
        deltas = pl.pallas_call(
            delta_kernel,
            out_shape=[part] * X,
            in_specs=[smem()] * 2 + [anywhere()] * (2 * Y) + [vmem()] * X,
            out_specs=[vmem()] * X,
            scratch_shapes=[
                pltpu.VMEM((SLOTS, b_rows, 128), BF16),
                pltpu.VMEM((SLOTS, b_rows, 128), BF16),
                pltpu.SemaphoreType.DMA((2, SLOTS)),
            ],
            compiler_params=PARAMS,
            name="deltas",
        )(ids, placement_map, *ups, *others, *chips)
        return tuple([deltas[0]] + [shift_x(deltas[k], -k) for k in range(1, X)])

    shifted = lax.cond(
        some,
        spread,
        zeros([part] * X),
        *(ids, placement_map, *arrived),
    )

    served = pl.pallas_call(
        merge_kernel,
        out_shape=jax.ShapeDtypeStruct((SLOTS, TILE_ROWS, width), BF16),
        in_specs=[smem()] * 2 + [vmem()] * (2 + X),
        out_specs=vmem(),
        compiler_params=PARAMS,
        name="merge",
    )(ids, placement_map, low, high, *shifted)

    return (
        new_a[None],
        new_a1[None],
        new_a2[None],
        new_b[None],
        new_b1[None],
        new_b2[None],
        served[:, None],
    )


def solution(mesh):
    return jax.shard_map(
        per_device,
        mesh=mesh,
        in_specs=(
            P("dp", "expert", None, None),
            P("dp", "expert", None, None),
            P(None, "expert"),
            P("expert", "dp", None),
            P("expert", "dp", None),
            P("expert", "dp", None),
            P("expert", None, "dp"),
            P("expert", None, "dp"),
            P("expert", None, "dp"),
            P("expert", "dp", None),
            P(),
        ),
        out_specs=(
            P("expert", "dp", None),
            P("expert", "dp", None),
            P("expert", "dp", None),
            P("expert", None, "dp"),
            P("expert", None, "dp"),
            P("expert", None, "dp"),
            P("expert", "dp", None, None),
        ),
        check_vma=False,
    )
```

```python
import jax
import jax.numpy as jnp
from jax import lax
from jax.experimental import pallas as pl
from jax.experimental.pallas import tpu as pltpu
from jax.sharding import PartitionSpec as P

LOW_RANK = 64
TILE_ROWS = 16
TILES = 32
SLOTS = 16
EARLY = 1
Z, Y, DP = 8, 4, 8
X = 4

beta_one = 0.9
beta_two = 0.95
learn_rate = 0.05
adam_eps = 1e-08
bias_one = 1.0 - 0.9**10
bias_two = 1.0 - 0.95**10
adapter_scale = 2.0

F32 = jnp.float32
BF16 = jnp.bfloat16


def adam_step(weights, moment_one, moment_two, gradient):
    moment_one = beta_one * moment_one + (1.0 - beta_one) * gradient
    moment_two = beta_two * moment_two + (1.0 - beta_two) * gradient * gradient
    update_step = (
        learn_rate * (moment_one / bias_one) / (jnp.sqrt(moment_two / bias_two) + adam_eps)
    )
    return (weights - update_step, moment_one, moment_two)


def shift_x(array, k):
    return lax.ppermute(
        array, "dp", [(i, (i // 2 + k) % X * 2 + i % 2) for i in range(DP)]
    )


def swap_core(array):
    return lax.ppermute(array, "dp", [(i, i // 2 * 2 + 1 - i % 2) for i in range(DP)])


def shift_y(array, k):
    return lax.ppermute(
        array, "expert", [(i, i // Y * Y + (i % Y + k) % Y) for i in range(Z * Y)]
    )


def vmem():
    return pl.BlockSpec(memory_space=pltpu.VMEM)


def smem():
    return pl.BlockSpec(memory_space=pltpu.SMEM)


def anywhere():
    return pl.BlockSpec(memory_space=pl.ANY)


PARAMS = pltpu.CompilerParams(vmem_limit_bytes=60 * 1024 * 1024)


def gradient_kernel(ids, counts, x, g, *refs):
    blocks, keep, give = refs[:DP], refs[DP], refs[DP + 1]
    chip, core = ids[0] // 2, lax.rem(ids[0], 2)
    live = counts[ids[0]]
    rows = x.shape[0]
    a_rows = x.shape[1] // DP
    cols = g.shape[1] // DP
    tiles = cols // 128
    projected = jnp.zeros((rows, 2 * LOW_RANK), F32)
    gate = jnp.zeros((rows, LOW_RANK), F32)
    up = jnp.zeros((rows, LOW_RANK), F32)
    for i in range(DP):
        k, c = i // 2, i % 2
        j = 2 * lax.rem(chip + X - k, X) + (1 - core if c else core)
        part = x[:, pl.ds(pl.multiple_of(j * a_rows, a_rows), a_rows)]
        projected += jnp.dot(part, blocks[i][:a_rows, :], preferred_element_type=F32)
        b_block = jnp.concatenate(
            [
                blocks[i][a_rows + t * LOW_RANK : a_rows + (t + 1) * LOW_RANK, :]
                for t in range(tiles)
            ],
            axis=1,
        )
        part = g[:, pl.ds(pl.multiple_of(j * cols, 128), cols)]
        term = lax.dot_general(
            part, b_block, (((1,), (1,)), ((), ())), preferred_element_type=F32
        )
        is_gate = j < DP // 2
        gate += jnp.where(is_gate, term, 0.0)
        up += jnp.where(is_gate, 0.0, term)
    mask = lax.broadcasted_iota(jnp.int32, (rows, 2 * LOW_RANK), 0) < live
    backward = jnp.where(mask, jnp.concatenate([gate, up], axis=1), 0.0)
    backward_t = jnp.transpose(backward).astype(BF16)
    projected_t = jnp.transpose(jnp.where(mask, projected, 0.0)).astype(BF16)
    for i in range(DP):
        k, c = i // 2, i % 2
        j = 2 * lax.rem(chip + k, X) + (1 - core if c else core)
        out = give if c else keep
        part = x[:, pl.ds(pl.multiple_of(j * a_rows, a_rows), a_rows)]
        grad = jnp.dot(backward_t, part, preferred_element_type=F32).astype(BF16)
        for t in range(a_rows // 128):
            out[k, t * 128 : (t + 1) * 128, :] = grad[:, t * 128 : (t + 1) * 128]
        part = g[:, pl.ds(pl.multiple_of(j * cols, 128), cols)]
        half = jnp.where(j < DP // 2, projected_t[:LOW_RANK], projected_t[LOW_RANK:])
        grad = jnp.dot(half, part, preferred_element_type=F32).astype(BF16)
        for t in range(tiles):
            out[k, a_rows + t * LOW_RANK : a_rows + (t + 1) * LOW_RANK, :] = grad[
                :, t * 128 : (t + 1) * 128
            ]


def pack_kernel(a, b, out):
    a_rows = a.shape[0]
    out[:a_rows, :] = a[...].astype(BF16)
    for t in range(b.shape[1] // 128):
        r = slice(a_rows + t * LOW_RANK, a_rows + (t + 1) * LOW_RANK)
        out[r, :] = b[:, t * 128 : (t + 1) * 128].astype(BF16)


def pair_kernel(kept, taken, *outs):
    for k in range(X):
        outs[k][...] = (kept[k].astype(F32) + taken[k].astype(F32)).astype(BF16)


def adam_kernel(ids, pick, counts, *refs):
    blocks = refs[:X]
    a, a1, a2, b, b1, b2 = refs[X : X + 6]
    na, na1, na2, nb, nb1, nb2 = refs[X + 6 : X + 12]
    send, rest, rows, ah = refs[X + 12 :]
    tokens = counts[0]
    for p in range(1, DP):
        tokens += counts[p]
    factor = adapter_scale / jnp.full((1, 128), tokens, jnp.int32).astype(F32)
    a_rows = a.shape[0]

    def total(lo, hi):
        s = blocks[0][lo:hi, :].astype(F32)
        for k in range(1, X):
            s += blocks[k][lo:hi, :].astype(F32)
        return s * factor

    for t in range(b.shape[1] // 128):
        c = slice(t * 128, (t + 1) * 128)
        grad = total(a_rows + t * LOW_RANK, a_rows + (t + 1) * LOW_RANK)
        new, one, two = adam_step(b[:, c], b1[:, c], b2[:, c], grad)
        nb[:, c], nb1[:, c], nb2[:, c] = new, one, two
        if t < EARLY:
            for dz in range(Z):
                send[dz, t * LOW_RANK : (t + 1) * LOW_RANK, :] = new.astype(BF16)
        else:
            rest[(t - EARLY) * LOW_RANK : (t - EARLY + 1) * LOW_RANK, :] = new.astype(BF16)
    for t in range(a_rows // 128):
        r = slice(t * 128, (t + 1) * 128)
        grad = jnp.transpose(total(t * 128, (t + 1) * 128))
        new, one, two = adam_step(a[r, :], a1[r, :], a2[r, :], grad)
        na[r, :], na1[r, :], na2[r, :] = new, one, two
        ah[r, :] = new.astype(BF16)
    for owner in range(Z * Y):
        start = pl.multiple_of(pick[owner] * TILE_ROWS, TILE_ROWS)
        rows[owner * TILE_ROWS : (owner + 1) * TILE_ROWS, :] = ah[pl.ds(start, TILE_ROWS), :]
    y = lax.rem(ids[1], Y)
    for dz in range(Z):
        for dy in range(Y):
            owner = dz * Y + lax.rem(y + dy, Y)
            start = pl.multiple_of(owner * TILE_ROWS, TILE_ROWS)
            first = EARLY * LOW_RANK + dy * TILE_ROWS
            send[dz, first : first + TILE_ROWS, :] = rows[pl.ds(start, TILE_ROWS), :]


def tiles_kernel(pick, frozen, early, late, whole, sem):
    copies = []
    for owner in range(Z * Y):
        rows = pl.ds(pl.multiple_of(pick[owner] * TILE_ROWS, TILE_ROWS), TILE_ROWS)
        copies.append(
            pltpu.make_async_copy(frozen.at[rows, :], whole.at[owner], sem.at[owner])
        )
        copies[owner].start()
    cols, one, two = whole.shape[2] // DP, early.shape[2] // DP, late.shape[2] // DP
    for owner in range(Z * Y):
        copies[owner].wait()
        for j in range(DP):
            tile = whole[owner, :, j * cols : (j + 1) * cols]
            early[owner, :, j * one : (j + 1) * one] = tile[:, :one]
            late[owner, :, j * two : (j + 1) * two] = tile[:, one:]


def mix_kernel(ids, late, rows, *refs):
    blocks, out = refs[:DP], refs[DP]
    chip, core = ids[0] // 2, lax.rem(ids[0], 2)
    cols = out.shape[2] // DP
    for i in range(DP):
        k, c = i // 2, i % 2
        j = 2 * lax.rem(chip + X - k, X) + (1 - core if c else core)
        left = jnp.where(j < DP // 2, rows[:, :LOW_RANK], rows[:, LOW_RANK:])
        for t in range(cols // 128):
            right = blocks[i][t * LOW_RANK : (t + 1) * LOW_RANK, :]
            delta = adapter_scale * jnp.dot(left, right, preferred_element_type=F32)
            span = pl.ds(pl.multiple_of(j * cols + t * 128, 128), 128)
            base = late[:, :, span].astype(F32)
            out[:, :, span] = (base + delta.reshape(base.shape)).astype(BF16)


def stack_kernel(arrived, *outs):
    b_rows = arrived.shape[1] - Y * TILE_ROWS
    for dy, out in enumerate(outs):
        first = b_rows + dy * TILE_ROWS
        out[:, :b_rows, :] = arrived[:, :b_rows, :]
        out[:, b_rows:, :] = arrived[:, first : first + TILE_ROWS, :]


def rows_kernel(*refs):
    parts, out = refs[:Y], refs[Y]
    b_rows = parts[0].shape[1] - TILE_ROWS
    for dy, part in enumerate(parts):
        out[dy] = part[:, b_rows:, :]


def slot_of(ids, table, s):
    source = table[ids[1] * SLOTS + s] // TILES
    dz = source // Y
    dy = lax.rem(lax.rem(ids[1], Y) + Y - lax.rem(source, Y), Y)
    return source, dz, dy


def delta_kernel(ids, table, *refs):
    ups, others, downs = refs[:Y], refs[Y : 2 * Y], refs[2 * Y : 2 * Y + X]
    outs, (own, other, sem) = refs[2 * Y + X : 2 * Y + 2 * X], refs[2 * Y + 2 * X :]
    n_tiles = own.shape[1] // LOW_RANK
    cols = n_tiles * 128
    chip, core = ids[0] // 2, lax.rem(ids[0], 2)
    up = pl.ds(0, own.shape[1])
    places = []
    for s in range(SLOTS):
        _, dz, dy = slot_of(ids, table, s)
        places.append((dy, dz))
        for i in range(Y):

            @pl.when(dy == i)
            def _(s=s, i=i, dz=dz):
                pltpu.make_async_copy(ups[i].at[dz, up], own.at[s], sem.at[0, s]).start()
                pltpu.make_async_copy(others[i].at[dz, up], other.at[s], sem.at[1, s]).start()

    for s in range(SLOTS):
        pltpu.make_async_copy(ups[0].at[0, up], own.at[s], sem.at[0, s]).wait()
        pltpu.make_async_copy(others[0].at[0, up], other.at[s], sem.at[1, s]).wait()
    is_gate = chip < X // 2
    spans = [pl.ds(pl.multiple_of(c * cols, 128), cols) for c in (core, 1 - core)]
    for s in range(SLOTS):
        left = jnp.concatenate([downs[k][places[s]] for k in range(X)], axis=0)
        left = jnp.where(is_gate, left[:, :LOW_RANK], left[:, LOW_RANK:])
        for ref, span in zip((own, other), spans):
            right = jnp.concatenate(
                [ref[s, t * LOW_RANK : (t + 1) * LOW_RANK, :] for t in range(n_tiles)], axis=1
            )
            delta = adapter_scale * jnp.dot(left, right, preferred_element_type=F32)
            delta = delta.astype(BF16)
            for k in range(X):
                outs[k][s, :, span] = delta[k * TILE_ROWS : (k + 1) * TILE_ROWS]


def merge_kernel(ids, table, early, late, *refs):
    deltas, out = refs[:X], refs[X]
    chip = ids[0] // 2
    one, two = early.shape[2] // DP, late.shape[2] // DP
    for s in range(SLOTS):
        source = table[ids[1] * SLOTS + s] // TILES
        for k in range(X):
            for c in range(2):
                j = 2 * lax.rem(chip + k, X) + c
                span = pl.ds(pl.multiple_of(j * one, 128), one)
                new = early[source, :, span].astype(F32)
                new += deltas[k][s, :, c * one : (c + 1) * one].astype(F32)
                start = pl.multiple_of(j * (one + two), 128)
                out[s, :, pl.ds(start, one)] = new.astype(BF16)
        for j in range(DP):
            start = j * (one + two) + one
            out[s, :, start : start + two] = late[source, :, j * two : (j + 1) * two]


def per_device(
    x_rows,
    out_grads,
    token_counts,
    a_param,
    a_first,
    a_second,
    b_param,
    b_first,
    b_second,
    frozen_tiles,
    placement_map,
):
    dp, expert = lax.axis_index("dp"), lax.axis_index("expert")
    ids = jnp.stack([dp, expert]).astype(jnp.int32)
    x, g = x_rows[0, 0], out_grads[0, 0]
    a, a1, a2 = a_param[0], a_first[0], a_second[0]
    b, b1, b2 = b_param[0], b_first[0], b_second[0]
    frozen = frozen_tiles[0]
    counts = token_counts.reshape(DP)
    a_rows, width = a.shape[0], frozen.shape[1]
    cols = b.shape[1]
    shape_a, shape_b = jax.ShapeDtypeStruct(a.shape, F32), jax.ShapeDtypeStruct(b.shape, F32)
    shape_block = jax.ShapeDtypeStruct((a_rows + cols // 128 * LOW_RANK, 128), BF16)

    table = placement_map.reshape(Z * Y, SLOTS)
    pick = jnp.sum(jnp.where(table // TILES == expert, table % TILES, 0), axis=1)
    n_tiles = cols // 128
    sizes = [DP * EARLY * 128, DP * (n_tiles - EARLY) * 128]
    halves = [jax.ShapeDtypeStruct((Z * Y, TILE_ROWS, n), BF16) for n in sizes]
    some = dp < DP

    def zeros(shapes):
        return lambda *_: tuple(jnp.zeros(s.shape, s.dtype) for s in shapes)

    def begin(a, b, pick, frozen):
        block = pl.pallas_call(
            pack_kernel,
            out_shape=shape_block,
            in_specs=[vmem()] * 2,
            out_specs=vmem(),
            compiler_params=PARAMS,
            name="pack",
        )(a, b)
        chips = [block] + [shift_x(block, k) for k in range(1, X)]
        tiles = pl.pallas_call(
            tiles_kernel,
            out_shape=halves,
            in_specs=[smem(), anywhere()],
            out_specs=[vmem()] * 2,
            scratch_shapes=[
                pltpu.VMEM((Z * Y, TILE_ROWS, width), BF16),
                pltpu.SemaphoreType.DMA((Z * Y,)),
            ],
            compiler_params=PARAMS,
            cost_estimate=pl.CostEstimate(
                flops=0, bytes_accessed=16 * Z * Y * TILE_ROWS * width, transcendentals=0
            ),
            name="tiles",
        )(pick, frozen)
        tiles, chips[-1] = lax.optimization_barrier((tiles, chips[-1]))
        blocks = [b for mine in chips for b in (mine, swap_core(mine))]
        return (*tiles, *blocks)

    early_out, late_base, *blocks = lax.cond(
        some, begin, zeros(halves + [shape_block] * DP), a, b, pick, frozen
    )
    early = lax.all_to_all(early_out, "expert", split_axis=0, concat_axis=0, tiled=True)
    rest = jax.ShapeDtypeStruct(((n_tiles - EARLY) * LOW_RANK, 128), BF16)
    rows = jax.ShapeDtypeStruct((Z * Y * TILE_ROWS, 128), BF16)

    def update(x, g, a, a1, a2, b, b1, b2, ids, pick, counts, *blocks):
        kept, given = pl.pallas_call(
            gradient_kernel,
            out_shape=[jax.ShapeDtypeStruct((X,) + shape_block.shape, BF16)] * 2,
            in_specs=[smem()] * 2 + [vmem()] * (2 + DP),
            out_specs=[vmem()] * 2,
            compiler_params=PARAMS,
            name="gradients",
        )(ids, counts, x, g, *blocks)
        taken = swap_core(given)
        pairs = pl.pallas_call(
            pair_kernel,
            out_shape=[shape_block] * X,
            in_specs=[vmem()] * 2,
            out_specs=[vmem()] * X,
            compiler_params=PARAMS,
            name="pairs",
        )(kept, taken)
        sums = [pairs[0]] + [shift_x(pairs[k], k) for k in range(1, X)]

        new_a, new_a1, new_a2, new_b, new_b1, new_b2, messages, b_rest, a_rows = pl.pallas_call(
            adam_kernel,
            out_shape=[shape_a] * 3 + [shape_b] * 3 + [message, rest, rows],
            in_specs=[smem()] * 3 + [vmem()] * (X + 6),
            out_specs=[vmem()] * 9,
            scratch_shapes=[pltpu.VMEM(a.shape, BF16)],
            compiler_params=PARAMS,
            name="adam",
        )(ids, pick, counts, *sums, a, a1, a2, b, b1, b2)
        return (new_a, new_a1, new_a2, new_b, new_b1, new_b2, messages, b_rest, a_rows)

    b_rows = EARLY * LOW_RANK
    message = jax.ShapeDtypeStruct((Z, b_rows + Y * TILE_ROWS, 128), BF16)
    part = jax.ShapeDtypeStruct((SLOTS, TILE_ROWS, 2 * EARLY * 128), BF16)

    outs = lax.cond(
        some,
        update,
        zeros([shape_a] * 3 + [shape_b] * 3 + [message, rest, rows]),
        *(x, g, a, a1, a2, b, b1, b2, ids, pick, counts, *blocks),
    )
    new_a, new_a1, new_a2, new_b, new_b1, new_b2 = outs[:6]

    messages, b_rest, a_rows = outs[6:]
    chips = [b_rest] + [shift_x(b_rest, k) for k in range(1, X)]
    messages, early = lax.optimization_barrier((messages, early))
    arrived = lax.all_to_all(
        messages,
        "expert",
        split_axis=0,
        concat_axis=0,
        tiled=True,
        axis_index_groups=[[z * Y + y for z in range(Z)] for y in range(Y)],
    )
    others = [b for mine in chips for b in (mine, swap_core(mine))]
    mixed = pl.pallas_call(
        mix_kernel,
        out_shape=jax.ShapeDtypeStruct(late_base.shape, BF16),
        in_specs=[smem()] + [vmem()] * (2 + DP),
        out_specs=vmem(),
        compiler_params=PARAMS,
        name="mix",
    )(ids, late_base, a_rows, *others)
    mixed, arrived = lax.optimization_barrier((mixed, arrived))
    late = lax.all_to_all(mixed, "expert", split_axis=0, concat_axis=0, tiled=True)

    def spread(ids, placement_map, arrived):
        parts = pl.pallas_call(
            stack_kernel,
            out_shape=[jax.ShapeDtypeStruct((Z, b_rows + TILE_ROWS, 128), BF16)] * Y,
            in_specs=[vmem()],
            out_specs=[vmem()] * Y,
            compiler_params=PARAMS,
            name="stack",
        )(arrived)
        ups = [parts[0]] + [shift_y(parts[dy], dy) for dy in range(1, Y)]
        rows = pl.pallas_call(
            rows_kernel,
            out_shape=jax.ShapeDtypeStruct((Y, Z, TILE_ROWS, 128), BF16),
            in_specs=[vmem()] * Y,
            out_specs=vmem(),
            compiler_params=PARAMS,
            name="rows",
        )(*ups)
        chips = [rows] + [shift_x(rows, k) for k in range(1, X)]
        others = [swap_core(u) for u in ups]
        deltas = pl.pallas_call(
            delta_kernel,
            out_shape=[part] * X,
            in_specs=[smem()] * 2 + [anywhere()] * (2 * Y) + [vmem()] * X,
            out_specs=[vmem()] * X,
            scratch_shapes=[
                pltpu.VMEM((SLOTS, b_rows, 128), BF16),
                pltpu.VMEM((SLOTS, b_rows, 128), BF16),
                pltpu.SemaphoreType.DMA((2, SLOTS)),
            ],
            compiler_params=PARAMS,
            name="deltas",
        )(ids, placement_map, *ups, *others, *chips)
        return tuple([deltas[0]] + [shift_x(deltas[k], -k) for k in range(1, X)])

    shifted = lax.cond(
        some,
        spread,
        zeros([part] * X),
        *(ids, placement_map, arrived),
    )

    served = pl.pallas_call(
        merge_kernel,
        out_shape=jax.ShapeDtypeStruct((SLOTS, TILE_ROWS, width), BF16),
        in_specs=[smem()] * 2 + [vmem()] * (2 + X),
        out_specs=vmem(),
        compiler_params=PARAMS,
        name="merge",
    )(ids, placement_map, early, late, *shifted)

    return (
        new_a[None],
        new_a1[None],
        new_a2[None],
        new_b[None],
        new_b1[None],
        new_b2[None],
        served[:, None],
    )


def solution(mesh):
    return jax.shard_map(
        per_device,
        mesh=mesh,
        in_specs=(
            P("dp", "expert", None, None),
            P("dp", "expert", None, None),
            P(None, "expert"),
            P("expert", "dp", None),
            P("expert", "dp", None),
            P("expert", "dp", None),
            P("expert", None, "dp"),
            P("expert", None, "dp"),
            P("expert", None, "dp"),
            P("expert", "dp", None),
            P(),
        ),
        out_specs=(
            P("expert", "dp", None),
            P("expert", "dp", None),
            P("expert", "dp", None),
            P("expert", None, "dp"),
            P("expert", None, "dp"),
            P("expert", None, "dp"),
            P("expert", "dp", None, None),
        ),
        check_vma=False,
    )
```

```python
import functools

import jax
import jax.numpy as jnp
from jax import lax
from jax.experimental import pallas as pl
from jax.experimental.pallas import tpu as pltpu
from jax.sharding import PartitionSpec as P

LOW_RANK = 64
TILE_ROWS = 16
TILES = 32
SLOTS = 16
EARLY = 1
LONG = 10**12
Z, Y, DP = 8, 4, 8
X = 4

beta_one = 0.9
beta_two = 0.95
learn_rate = 0.05
adam_eps = 1e-08
bias_one = 1.0 - 0.9**10
bias_two = 1.0 - 0.95**10
adapter_scale = 2.0

F32 = jnp.float32
BF16 = jnp.bfloat16


def adam_step(weights, moment_one, moment_two, gradient):
    moment_one = beta_one * moment_one + (1.0 - beta_one) * gradient
    moment_two = beta_two * moment_two + (1.0 - beta_two) * gradient * gradient
    update_step = (
        learn_rate * (moment_one / bias_one) / (jnp.sqrt(moment_two / bias_two) + adam_eps)
    )
    return (weights - update_step, moment_one, moment_two)


def shift_x(array, k):
    return lax.ppermute(
        array, "dp", [(i, (i // 2 + k) % X * 2 + i % 2) for i in range(DP)]
    )


def swap_core(array):
    return lax.ppermute(array, "dp", [(i, i // 2 * 2 + 1 - i % 2) for i in range(DP)])


def shift_y(array, k):
    return lax.ppermute(
        array, "expert", [(i, i // Y * Y + (i % Y + k) % Y) for i in range(Z * Y)]
    )


def vmem():
    return pl.BlockSpec(memory_space=pltpu.VMEM)


def smem():
    return pl.BlockSpec(memory_space=pltpu.SMEM)


def anywhere():
    return pl.BlockSpec(memory_space=pl.ANY)


PARAMS = pltpu.CompilerParams(vmem_limit_bytes=60 * 1024 * 1024)
HEAVY = pl.CostEstimate(flops=LONG, bytes_accessed=LONG // 100, transcendentals=0)


def gradient_kernel(ids, counts, x, g, *refs):
    blocks, keep, give = refs[:DP], refs[DP], refs[DP + 1]
    chip, core = ids[0] // 2, lax.rem(ids[0], 2)
    live = counts[ids[0]]
    rows = x.shape[0]
    a_rows = x.shape[1] // DP
    cols = g.shape[1] // DP
    tiles = cols // 128
    projected = jnp.zeros((rows, 2 * LOW_RANK), F32)
    gate = jnp.zeros((rows, LOW_RANK), F32)
    up = jnp.zeros((rows, LOW_RANK), F32)
    for i in range(DP):
        k, c = i // 2, i % 2
        j = 2 * lax.rem(chip + X - k, X) + (1 - core if c else core)
        part = x[:, pl.ds(pl.multiple_of(j * a_rows, a_rows), a_rows)]
        projected += jnp.dot(part, blocks[i][:a_rows, :], preferred_element_type=F32)
        b_block = jnp.concatenate(
            [
                blocks[i][a_rows + t * LOW_RANK : a_rows + (t + 1) * LOW_RANK, :]
                for t in range(tiles)
            ],
            axis=1,
        )
        part = g[:, pl.ds(pl.multiple_of(j * cols, 128), cols)]
        term = lax.dot_general(
            part, b_block, (((1,), (1,)), ((), ())), preferred_element_type=F32
        )
        is_gate = j < DP // 2
        gate += jnp.where(is_gate, term, 0.0)
        up += jnp.where(is_gate, 0.0, term)
    mask = lax.broadcasted_iota(jnp.int32, (rows, 2 * LOW_RANK), 0) < live
    backward = jnp.where(mask, jnp.concatenate([gate, up], axis=1), 0.0)
    backward_t = jnp.transpose(backward).astype(BF16)
    projected_t = jnp.transpose(jnp.where(mask, projected, 0.0)).astype(BF16)
    for i in range(DP):
        k, c = i // 2, i % 2
        j = 2 * lax.rem(chip + k, X) + (1 - core if c else core)
        out = give if c else keep
        part = x[:, pl.ds(pl.multiple_of(j * a_rows, a_rows), a_rows)]
        grad = jnp.dot(backward_t, part, preferred_element_type=F32).astype(BF16)
        for t in range(a_rows // 128):
            out[k, t * 128 : (t + 1) * 128, :] = grad[:, t * 128 : (t + 1) * 128]
        part = g[:, pl.ds(pl.multiple_of(j * cols, 128), cols)]
        half = jnp.where(j < DP // 2, projected_t[:LOW_RANK], projected_t[LOW_RANK:])
        grad = jnp.dot(half, part, preferred_element_type=F32).astype(BF16)
        for t in range(tiles):
            out[k, a_rows + t * LOW_RANK : a_rows + (t + 1) * LOW_RANK, :] = grad[
                :, t * 128 : (t + 1) * 128
            ]


def pack_kernel(a, b, out):
    a_rows = a.shape[0]
    out[:a_rows, :] = a[...].astype(BF16)
    for t in range(b.shape[1] // 128):
        r = slice(a_rows + t * LOW_RANK, a_rows + (t + 1) * LOW_RANK)
        out[r, :] = b[:, t * 128 : (t + 1) * 128].astype(BF16)


def pair_kernel(kept, taken, *outs):
    for k in range(X):
        outs[k][...] = (kept[k].astype(F32) + taken[k].astype(F32)).astype(BF16)


def adam_kernel(ids, pick, counts, *refs):
    blocks = refs[:X]
    a, a1, a2, b, b1, b2 = refs[X : X + 6]
    na, na1, na2, nb, nb1, nb2 = refs[X + 6 : X + 12]
    send, rest, rows, ah = refs[X + 12 :]
    tokens = counts[0]
    for p in range(1, DP):
        tokens += counts[p]
    factor = adapter_scale / jnp.full((1, 128), tokens, jnp.int32).astype(F32)
    a_rows = a.shape[0]

    def total(lo, hi):
        s = blocks[0][lo:hi, :].astype(F32)
        for k in range(1, X):
            s += blocks[k][lo:hi, :].astype(F32)
        return s * factor

    for t in range(b.shape[1] // 128):
        c = slice(t * 128, (t + 1) * 128)
        grad = total(a_rows + t * LOW_RANK, a_rows + (t + 1) * LOW_RANK)
        new, one, two = adam_step(b[:, c], b1[:, c], b2[:, c], grad)
        nb[:, c], nb1[:, c], nb2[:, c] = new, one, two
        if t < EARLY:
            for dz in range(Z):
                send[dz, t * LOW_RANK : (t + 1) * LOW_RANK, :] = new.astype(BF16)
        else:
            rest[(t - EARLY) * LOW_RANK : (t - EARLY + 1) * LOW_RANK, :] = new.astype(BF16)
    for t in range(a_rows // 128):
        r = slice(t * 128, (t + 1) * 128)
        grad = jnp.transpose(total(t * 128, (t + 1) * 128))
        new, one, two = adam_step(a[r, :], a1[r, :], a2[r, :], grad)
        na[r, :], na1[r, :], na2[r, :] = new, one, two
        ah[r, :] = new.astype(BF16)
    for owner in range(Z * Y):
        start = pl.multiple_of(pick[owner] * TILE_ROWS, TILE_ROWS)
        rows[owner * TILE_ROWS : (owner + 1) * TILE_ROWS, :] = ah[pl.ds(start, TILE_ROWS), :]
    y = lax.rem(ids[1], Y)
    for dz in range(Z):
        for dy in range(Y):
            owner = dz * Y + lax.rem(y + dy, Y)
            start = pl.multiple_of(owner * TILE_ROWS, TILE_ROWS)
            first = EARLY * LOW_RANK + dy * TILE_ROWS
            send[dz, first : first + TILE_ROWS, :] = rows[pl.ds(start, TILE_ROWS), :]


def tiles_kernel(first, pick, frozen, out, whole, sem):
    copies = []
    for owner in range(Z * Y):
        rows = pl.ds(pl.multiple_of(pick[owner] * TILE_ROWS, TILE_ROWS), TILE_ROWS)
        copies.append(
            pltpu.make_async_copy(frozen.at[rows, :], whole.at[owner], sem.at[owner])
        )
        copies[owner].start()
    cols, part = whole.shape[2] // DP, out.shape[2] // DP
    for owner in range(Z * Y):
        copies[owner].wait()
        for j in range(DP):
            start = j * cols + first
            out[owner, :, j * part : (j + 1) * part] = whole[owner, :, start : start + part]


def choose_tiles(first, cols, pick, frozen):
    shape = (Z * Y, TILE_ROWS, DP * cols)
    return pl.pallas_call(
        functools.partial(tiles_kernel, first),
        out_shape=jax.ShapeDtypeStruct(shape, BF16),
        in_specs=[smem(), anywhere()],
        out_specs=vmem(),
        scratch_shapes=[
            pltpu.VMEM((Z * Y, TILE_ROWS, frozen.shape[1]), BF16),
            pltpu.SemaphoreType.DMA((Z * Y,)),
        ],
        compiler_params=PARAMS,
        name="tiles",
    )(pick, frozen)


def mix_kernel(ids, late, rows, *refs):
    blocks, out = refs[:DP], refs[DP]
    chip, core = ids[0] // 2, lax.rem(ids[0], 2)
    cols = out.shape[2] // DP
    for i in range(DP):
        k, c = i // 2, i % 2
        j = 2 * lax.rem(chip + X - k, X) + (1 - core if c else core)
        left = jnp.where(j < DP // 2, rows[:, :LOW_RANK], rows[:, LOW_RANK:])
        for t in range(cols // 128):
            right = blocks[i][t * LOW_RANK : (t + 1) * LOW_RANK, :]
            delta = adapter_scale * jnp.dot(left, right, preferred_element_type=F32)
            span = pl.ds(pl.multiple_of(j * cols + t * 128, 128), 128)
            base = late[:, :, span].astype(F32)
            out[:, :, span] = (base + delta.reshape(base.shape)).astype(BF16)


def stack_kernel(arrived, *outs):
    b_rows = arrived.shape[1] - Y * TILE_ROWS
    for dy, out in enumerate(outs):
        first = b_rows + dy * TILE_ROWS
        out[:, :b_rows, :] = arrived[:, :b_rows, :]
        out[:, b_rows:, :] = arrived[:, first : first + TILE_ROWS, :]


def slot_of(ids, table, s):
    source = table[ids[1] * SLOTS + s] // TILES
    dz = source // Y
    dy = lax.rem(lax.rem(ids[1], Y) + Y - lax.rem(source, Y), Y)
    return source, dz, dy


def select_kernel(ids, table, *refs):
    parts, ups, downs = refs[:Y], refs[Y], refs[Y + 1]
    b_rows = ups.shape[1]
    for s in range(SLOTS):
        _, z, dy = slot_of(ids, table, s)
        for i in range(Y):

            @pl.when(dy == i)
            def _(s=s, i=i, z=z):
                ups[s] = parts[i][z, :b_rows, :]
                downs[s] = parts[i][z, b_rows:, :]


def early_kernel(ids, table, early, downs, *refs):
    ups, out = refs[:DP], refs[DP]
    chip, core = ids[0] // 2, lax.rem(ids[0], 2)
    sources = [slot_of(ids, table, s)[0] for s in range(SLOTS)]
    for i in range(DP):
        k, c = i // 2, i % 2
        j = 2 * lax.rem(chip + X - k, X) + (1 - core if c else core)
        is_gate = j < DP // 2
        for s in range(SLOTS):
            left = jnp.where(is_gate, downs[s, :, :LOW_RANK], downs[s, :, LOW_RANK:])
            for t in range(EARLY):
                right = ups[i][s, t * LOW_RANK : (t + 1) * LOW_RANK, :]
                delta = adapter_scale * jnp.dot(left, right, preferred_element_type=F32)
                span = pl.ds(pl.multiple_of((j * EARLY + t) * 128, 128), 128)
                base = early[sources[s], :, span].astype(F32)
                out[s, :, span] = (base + delta).astype(BF16)


def merge_kernel(ids, table, early, late, out):
    one, two = early.shape[2] // DP, late.shape[2] // DP
    for s in range(SLOTS):
        source = slot_of(ids, table, s)[0]
        for j in range(DP):
            start = j * (one + two)
            out[s, :, start : start + one] = early[s, :, j * one : (j + 1) * one]
            start += one
            out[s, :, start : start + two] = late[source, :, j * two : (j + 1) * two]


def per_device(
    x_rows,
    out_grads,
    token_counts,
    a_param,
    a_first,
    a_second,
    b_param,
    b_first,
    b_second,
    frozen_tiles,
    placement_map,
):
    dp, expert = lax.axis_index("dp"), lax.axis_index("expert")
    ids = jnp.stack([dp, expert]).astype(jnp.int32)
    x, g = x_rows[0, 0], out_grads[0, 0]
    a, a1, a2 = a_param[0], a_first[0], a_second[0]
    b, b1, b2 = b_param[0], b_first[0], b_second[0]
    frozen = frozen_tiles[0]
    counts = token_counts.reshape(DP)
    a_rows, width = a.shape[0], frozen.shape[1]
    cols = b.shape[1]
    shape_a, shape_b = jax.ShapeDtypeStruct(a.shape, F32), jax.ShapeDtypeStruct(b.shape, F32)
    shape_block = jax.ShapeDtypeStruct((a_rows + cols // 128 * LOW_RANK, 128), BF16)

    n_tiles = cols // 128
    sizes = [DP * EARLY * 128, DP * (n_tiles - EARLY) * 128]
    halves = [jax.ShapeDtypeStruct((Z * Y, TILE_ROWS, n), BF16) for n in sizes]
    some = dp < DP

    def zeros(shapes):
        return lambda *_: tuple(jnp.zeros(s.shape, s.dtype) for s in shapes)

    block = pl.pallas_call(
        pack_kernel,
        out_shape=shape_block,
        in_specs=[vmem()] * 2,
        out_specs=vmem(),
        compiler_params=PARAMS,
        name="pack",
    )(a, b)
    chips = [block] + [shift_x(block, k) for k in range(1, X)]

    table = placement_map.reshape(Z * Y, SLOTS)
    pick = jnp.sum(jnp.where(table // TILES == expert, table % TILES, 0), axis=1)
    early_out = choose_tiles(0, EARLY * 128, pick, frozen)
    early = lax.all_to_all(early_out, "expert", split_axis=0, concat_axis=0, tiled=True)
    rest = jax.ShapeDtypeStruct(((n_tiles - EARLY) * LOW_RANK, 128), BF16)
    rows = jax.ShapeDtypeStruct((Z * Y * TILE_ROWS, 128), BF16)

    def gradients(x, g, ids, counts, *chips):
        blocks = [b for mine in chips for b in (mine, swap_core(mine))]
        kept, given = pl.pallas_call(
            gradient_kernel,
            out_shape=[shape_blocks] * 2,
            in_specs=[smem()] * 2 + [vmem()] * (2 + DP),
            out_specs=[vmem()] * 2,
            compiler_params=PARAMS,
            name="gradients",
        )(ids, counts, x, g, *blocks)
        return kept, swap_core(given)

    shape_blocks = jax.ShapeDtypeStruct((X,) + shape_block.shape, BF16)
    kept, taken = lax.cond(
        some, gradients, zeros([shape_blocks] * 2), x, g, ids, counts, *chips
    )
    pairs = pl.pallas_call(
        pair_kernel,
        out_shape=[shape_block] * X,
        in_specs=[vmem()] * 2,
        out_specs=[vmem()] * X,
        compiler_params=PARAMS,
        cost_estimate=HEAVY,
        name="pairs",
    )(kept, taken)
    sums = [pairs[0]] + [shift_x(pairs[k], k) for k in range(1, X)]
    late_base = choose_tiles(EARLY * 128, (n_tiles - EARLY) * 128, pick, frozen)
    sums[-1], late_base = lax.optimization_barrier((sums[-1], late_base))
    b_rows = EARLY * LOW_RANK
    message = jax.ShapeDtypeStruct((Z, b_rows + Y * TILE_ROWS, 128), BF16)
    new_a, new_a1, new_a2, new_b, new_b1, new_b2, messages, b_rest, a_rows = pl.pallas_call(
        adam_kernel,
        out_shape=[shape_a] * 3 + [shape_b] * 3 + [message, rest, rows],
        in_specs=[smem()] * 3 + [vmem()] * (X + 6),
        out_specs=[vmem()] * 9,
        scratch_shapes=[pltpu.VMEM(a.shape, BF16)],
        compiler_params=pltpu.CompilerParams(vmem_limit_bytes=12 * 1024 * 1024),
        name="adam",
    )(ids, pick, counts, *sums, a, a1, a2, b, b1, b2)
    chips = [b_rest] + [shift_x(b_rest, k) for k in range(1, X)]
    messages, early = lax.optimization_barrier((messages, early))
    arrived = lax.all_to_all(
        messages,
        "expert",
        split_axis=0,
        concat_axis=0,
        tiled=True,
        axis_index_groups=[[z * Y + y for z in range(Z)] for y in range(Y)],
    )

    def swap_all(*chips):
        return tuple(b for mine in chips for b in (mine, swap_core(mine)))

    others = lax.cond(some, swap_all, zeros([rest] * DP), *chips)
    mixed = pl.pallas_call(
        mix_kernel,
        out_shape=jax.ShapeDtypeStruct(late_base.shape, BF16),
        in_specs=[smem()] + [vmem()] * (2 + DP),
        out_specs=vmem(),
        compiler_params=pltpu.CompilerParams(vmem_limit_bytes=12 * 1024 * 1024),
        cost_estimate=pl.CostEstimate(flops=4680000000, bytes_accessed=15600000, transcendentals=0),
        name="mix",
    )(ids, late_base, a_rows, *others)
    mixed, arrived = lax.optimization_barrier((mixed, arrived))
    late = lax.all_to_all(mixed, "expert", split_axis=0, concat_axis=0, tiled=True)

    served_early = jax.ShapeDtypeStruct((SLOTS, TILE_ROWS, sizes[0]), BF16)

    def spread(ids, placement_map, early, arrived):
        parts = pl.pallas_call(
            stack_kernel,
            out_shape=[jax.ShapeDtypeStruct((Z, b_rows + TILE_ROWS, 128), BF16)] * Y,
            in_specs=[vmem()],
            out_specs=[vmem()] * Y,
            compiler_params=PARAMS,
            name="stack",
        )(arrived)
        parts = [parts[0]] + [shift_y(parts[dy], dy) for dy in range(1, Y)]
        ups, downs = pl.pallas_call(
            select_kernel,
            out_shape=[
                jax.ShapeDtypeStruct((SLOTS, b_rows, 128), BF16),
                jax.ShapeDtypeStruct((SLOTS, TILE_ROWS, 128), BF16),
            ],
            in_specs=[smem()] * 2 + [vmem()] * Y,
            out_specs=[vmem()] * 2,
            compiler_params=PARAMS,
            name="select",
        )(ids, placement_map, *parts)
        chips = [ups] + [shift_x(ups, k) for k in range(1, X)]
        every = [b for mine in chips for b in (mine, swap_core(mine))]
        return pl.pallas_call(
            early_kernel,
            out_shape=served_early,
            in_specs=[smem()] * 2 + [vmem()] * (2 + DP),
            out_specs=vmem(),
            compiler_params=PARAMS,
            name="early",
        )(ids, placement_map, early, downs, *every)

    def no_spread(*_):
        return jnp.zeros(served_early.shape, BF16)

    first = lax.cond(some, spread, no_spread, ids, placement_map, early, arrived)

    served = pl.pallas_call(
        merge_kernel,
        out_shape=jax.ShapeDtypeStruct((SLOTS, TILE_ROWS, width), BF16),
        in_specs=[smem()] * 2 + [vmem()] * 2,
        out_specs=vmem(),
        compiler_params=pltpu.CompilerParams(vmem_limit_bytes=12 * 1024 * 1024),
        name="merge",
    )(ids, placement_map, first, late)

    return (
        new_a[None],
        new_a1[None],
        new_a2[None],
        new_b[None],
        new_b1[None],
        new_b2[None],
        served[:, None],
    )


def solution(mesh):
    return jax.shard_map(
        per_device,
        mesh=mesh,
        in_specs=(
            P("dp", "expert", None, None),
            P("dp", "expert", None, None),
            P(None, "expert"),
            P("expert", "dp", None),
            P("expert", "dp", None),
            P("expert", "dp", None),
            P("expert", None, "dp"),
            P("expert", None, "dp"),
            P("expert", None, "dp"),
            P("expert", "dp", None),
            P(),
        ),
        out_specs=(
            P("expert", "dp", None),
            P("expert", "dp", None),
            P("expert", "dp", None),
            P("expert", None, "dp"),
            P("expert", None, "dp"),
            P("expert", None, "dp"),
            P("expert", "dp", None, None),
        ),
        check_vma=False,
    )
```

```python
import functools

import jax
import jax.numpy as jnp
from jax import lax
from jax.experimental import pallas as pl
from jax.experimental.pallas import tpu as pltpu
from jax.sharding import PartitionSpec as P

LOW_RANK = 64
TILE_ROWS = 16
TILES = 32
SLOTS = 16
EARLY = 1
LONG = 10**12
Z, Y, DP = 8, 4, 8
X = 4

beta_one = 0.9
beta_two = 0.95
learn_rate = 0.05
adam_eps = 1e-08
bias_one = 1.0 - 0.9**10
bias_two = 1.0 - 0.95**10
adapter_scale = 2.0

F32 = jnp.float32
BF16 = jnp.bfloat16


def adam_step(weights, moment_one, moment_two, gradient):
    moment_one = beta_one * moment_one + (1.0 - beta_one) * gradient
    moment_two = beta_two * moment_two + (1.0 - beta_two) * gradient * gradient
    update_step = (
        learn_rate * (moment_one / bias_one) / (jnp.sqrt(moment_two / bias_two) + adam_eps)
    )
    return (weights - update_step, moment_one, moment_two)


def shift_x(array, k):
    return lax.ppermute(
        array, "dp", [(i, (i // 2 + k) % X * 2 + i % 2) for i in range(DP)]
    )


def swap_core(array):
    return lax.ppermute(array, "dp", [(i, i // 2 * 2 + 1 - i % 2) for i in range(DP)])


def shift_y(array, k):
    return lax.ppermute(
        array, "expert", [(i, i // Y * Y + (i % Y + k) % Y) for i in range(Z * Y)]
    )


def vmem():
    return pl.BlockSpec(memory_space=pltpu.VMEM)


def smem():
    return pl.BlockSpec(memory_space=pltpu.SMEM)


def anywhere():
    return pl.BlockSpec(memory_space=pl.ANY)


PARAMS = pltpu.CompilerParams(vmem_limit_bytes=60 * 1024 * 1024)
HEAVY = pl.CostEstimate(flops=LONG, bytes_accessed=LONG // 100, transcendentals=0)


def gradient_kernel(ids, counts, x, g, *refs):
    blocks, keep, give = refs[:DP], refs[DP], refs[DP + 1]
    chip, core = ids[0] // 2, lax.rem(ids[0], 2)
    live = counts[ids[0]]
    rows = x.shape[0]
    a_rows = x.shape[1] // DP
    cols = g.shape[1] // DP
    tiles = cols // 128
    projected = jnp.zeros((rows, 2 * LOW_RANK), F32)
    gate = jnp.zeros((rows, LOW_RANK), F32)
    up = jnp.zeros((rows, LOW_RANK), F32)
    for i in range(DP):
        k, c = i // 2, i % 2
        j = 2 * lax.rem(chip + X - k, X) + (1 - core if c else core)
        part = x[:, pl.ds(pl.multiple_of(j * a_rows, a_rows), a_rows)]
        projected += jnp.dot(part, blocks[i][:a_rows, :], preferred_element_type=F32)
        b_block = jnp.concatenate(
            [
                blocks[i][a_rows + t * LOW_RANK : a_rows + (t + 1) * LOW_RANK, :]
                for t in range(tiles)
            ],
            axis=1,
        )
        part = g[:, pl.ds(pl.multiple_of(j * cols, 128), cols)]
        term = lax.dot_general(
            part, b_block, (((1,), (1,)), ((), ())), preferred_element_type=F32
        )
        is_gate = j < DP // 2
        gate += jnp.where(is_gate, term, 0.0)
        up += jnp.where(is_gate, 0.0, term)
    mask = lax.broadcasted_iota(jnp.int32, (rows, 2 * LOW_RANK), 0) < live
    backward = jnp.where(mask, jnp.concatenate([gate, up], axis=1), 0.0)
    backward_t = jnp.transpose(backward).astype(BF16)
    projected_t = jnp.transpose(jnp.where(mask, projected, 0.0)).astype(BF16)
    for i in range(DP):
        k, c = i // 2, i % 2
        j = 2 * lax.rem(chip + k, X) + (1 - core if c else core)
        out = give if c else keep
        part = x[:, pl.ds(pl.multiple_of(j * a_rows, a_rows), a_rows)]
        grad = jnp.dot(backward_t, part, preferred_element_type=F32).astype(BF16)
        for t in range(a_rows // 128):
            out[k, t * 128 : (t + 1) * 128, :] = grad[:, t * 128 : (t + 1) * 128]
        part = g[:, pl.ds(pl.multiple_of(j * cols, 128), cols)]
        half = jnp.where(j < DP // 2, projected_t[:LOW_RANK], projected_t[LOW_RANK:])
        grad = jnp.dot(half, part, preferred_element_type=F32).astype(BF16)
        for t in range(tiles):
            out[k, a_rows + t * LOW_RANK : a_rows + (t + 1) * LOW_RANK, :] = grad[
                :, t * 128 : (t + 1) * 128
            ]


def pack_kernel(a, b, out):
    a_rows = a.shape[0]
    out[:a_rows, :] = a[...].astype(BF16)
    for t in range(b.shape[1] // 128):
        r = slice(a_rows + t * LOW_RANK, a_rows + (t + 1) * LOW_RANK)
        out[r, :] = b[:, t * 128 : (t + 1) * 128].astype(BF16)


def pair_kernel(kept, taken, *outs):
    for k in range(X):
        outs[k][...] = (kept[k].astype(F32) + taken[k].astype(F32)).astype(BF16)


def adam_kernel(ids, pick, counts, *refs):
    blocks = refs[:X]
    a, a1, a2, b, b1, b2 = refs[X : X + 6]
    na, na1, na2, nb, nb1, nb2 = refs[X + 6 : X + 12]
    send, rest, rows, ah = refs[X + 12 :]
    tokens = counts[0]
    for p in range(1, DP):
        tokens += counts[p]
    factor = adapter_scale / jnp.full((1, 128), tokens, jnp.int32).astype(F32)
    a_rows = a.shape[0]

    def total(lo, hi):
        s = blocks[0][lo:hi, :].astype(F32)
        for k in range(1, X):
            s += blocks[k][lo:hi, :].astype(F32)
        return s * factor

    for t in range(b.shape[1] // 128):
        c = slice(t * 128, (t + 1) * 128)
        grad = total(a_rows + t * LOW_RANK, a_rows + (t + 1) * LOW_RANK)
        new, one, two = adam_step(b[:, c], b1[:, c], b2[:, c], grad)
        nb[:, c], nb1[:, c], nb2[:, c] = new, one, two
        if t < EARLY:
            for dz in range(Z):
                send[dz, t * LOW_RANK : (t + 1) * LOW_RANK, :] = new.astype(BF16)
        else:
            rest[(t - EARLY) * LOW_RANK : (t - EARLY + 1) * LOW_RANK, :] = new.astype(BF16)
    for t in range(a_rows // 128):
        r = slice(t * 128, (t + 1) * 128)
        grad = jnp.transpose(total(t * 128, (t + 1) * 128))
        new, one, two = adam_step(a[r, :], a1[r, :], a2[r, :], grad)
        na[r, :], na1[r, :], na2[r, :] = new, one, two
        ah[r, :] = new.astype(BF16)
    for owner in range(Z * Y):
        start = pl.multiple_of(pick[owner] * TILE_ROWS, TILE_ROWS)
        rows[owner * TILE_ROWS : (owner + 1) * TILE_ROWS, :] = ah[pl.ds(start, TILE_ROWS), :]
    y = lax.rem(ids[1], Y)
    for dz in range(Z):
        for dy in range(Y):
            owner = dz * Y + lax.rem(y + dy, Y)
            start = pl.multiple_of(owner * TILE_ROWS, TILE_ROWS)
            first = EARLY * LOW_RANK + dy * TILE_ROWS
            send[dz, first : first + TILE_ROWS, :] = rows[pl.ds(start, TILE_ROWS), :]


def tiles_kernel(first, pick, frozen, out):
    cols, part = frozen.shape[1] // DP, out.shape[2] // DP
    for owner in range(Z * Y):
        rows = pl.ds(pl.multiple_of(pick[owner] * TILE_ROWS, TILE_ROWS), TILE_ROWS)
        for j in range(DP):
            start = j * cols + first
            out[owner, :, j * part : (j + 1) * part] = frozen[rows, start : start + part]


def choose_tiles(first, cols, pick, frozen):
    shape = (Z * Y, TILE_ROWS, DP * cols)
    return pl.pallas_call(
        functools.partial(tiles_kernel, first),
        out_shape=jax.ShapeDtypeStruct(shape, BF16),
        in_specs=[smem(), vmem()],
        out_specs=vmem(),
        compiler_params=PARAMS,
        name="tiles",
    )(pick, frozen)


def mix_kernel(ids, late, rows, *refs):
    blocks, out = refs[:DP], refs[DP]
    chip, core = ids[0] // 2, lax.rem(ids[0], 2)
    cols = out.shape[2] // DP
    for i in range(DP):
        k, c = i // 2, i % 2
        j = 2 * lax.rem(chip + X - k, X) + (1 - core if c else core)
        left = jnp.where(j < DP // 2, rows[:, :LOW_RANK], rows[:, LOW_RANK:])
        for t in range(cols // 128):
            right = blocks[i][t * LOW_RANK : (t + 1) * LOW_RANK, :]
            delta = adapter_scale * jnp.dot(left, right, preferred_element_type=F32)
            span = pl.ds(pl.multiple_of(j * cols + t * 128, 128), 128)
            base = late[:, :, span].astype(F32)
            out[:, :, span] = (base + delta.reshape(base.shape)).astype(BF16)


def stack_kernel(arrived, *outs):
    b_rows = arrived.shape[1] - Y * TILE_ROWS
    for dy, out in enumerate(outs):
        first = b_rows + dy * TILE_ROWS
        out[:, :b_rows, :] = arrived[:, :b_rows, :]
        out[:, b_rows:, :] = arrived[:, first : first + TILE_ROWS, :]


def slot_of(ids, table, s):
    source = table[ids[1] * SLOTS + s] // TILES
    dz = source // Y
    dy = lax.rem(lax.rem(ids[1], Y) + Y - lax.rem(source, Y), Y)
    return source, dz, dy


def select_kernel(ids, table, *refs):
    parts, ups, downs = refs[:Y], refs[Y], refs[Y + 1]
    b_rows = ups.shape[1]
    for s in range(SLOTS):
        _, z, dy = slot_of(ids, table, s)
        for i in range(Y):

            @pl.when(dy == i)
            def _(s=s, i=i, z=z):
                ups[s] = parts[i][z, :b_rows, :]
                downs[s] = parts[i][z, b_rows:, :]


def early_kernel(ids, table, early, downs, *refs):
    ups, out = refs[:DP], refs[DP]
    chip, core = ids[0] // 2, lax.rem(ids[0], 2)
    sources = [slot_of(ids, table, s)[0] for s in range(SLOTS)]
    for i in range(DP):
        k, c = i // 2, i % 2
        j = 2 * lax.rem(chip + X - k, X) + (1 - core if c else core)
        is_gate = j < DP // 2
        for s in range(SLOTS):
            left = jnp.where(is_gate, downs[s, :, :LOW_RANK], downs[s, :, LOW_RANK:])
            for t in range(EARLY):
                right = ups[i][s, t * LOW_RANK : (t + 1) * LOW_RANK, :]
                delta = adapter_scale * jnp.dot(left, right, preferred_element_type=F32)
                span = pl.ds(pl.multiple_of((j * EARLY + t) * 128, 128), 128)
                base = early[sources[s], :, span].astype(F32)
                out[s, :, span] = (base + delta).astype(BF16)


def merge_kernel(ids, table, early, late, out):
    one, two = early.shape[2] // DP, late.shape[2] // DP
    for s in range(SLOTS):
        source = slot_of(ids, table, s)[0]
        for j in range(DP):
            start = j * (one + two)
            out[s, :, start : start + one] = early[s, :, j * one : (j + 1) * one]
            start += one
            out[s, :, start : start + two] = late[source, :, j * two : (j + 1) * two]


def per_device(
    x_rows,
    out_grads,
    token_counts,
    a_param,
    a_first,
    a_second,
    b_param,
    b_first,
    b_second,
    frozen_tiles,
    placement_map,
):
    dp, expert = lax.axis_index("dp"), lax.axis_index("expert")
    ids = jnp.stack([dp, expert]).astype(jnp.int32)
    x, g = x_rows[0, 0], out_grads[0, 0]
    a, a1, a2 = a_param[0], a_first[0], a_second[0]
    b, b1, b2 = b_param[0], b_first[0], b_second[0]
    frozen = frozen_tiles[0]
    counts = token_counts.reshape(DP)
    a_rows, width = a.shape[0], frozen.shape[1]
    cols = b.shape[1]
    shape_a, shape_b = jax.ShapeDtypeStruct(a.shape, F32), jax.ShapeDtypeStruct(b.shape, F32)
    shape_block = jax.ShapeDtypeStruct((a_rows + cols // 128 * LOW_RANK, 128), BF16)

    n_tiles = cols // 128
    sizes = [DP * EARLY * 128, DP * (n_tiles - EARLY) * 128]
    halves = [jax.ShapeDtypeStruct((Z * Y, TILE_ROWS, n), BF16) for n in sizes]
    some = dp < DP

    def zeros(shapes):
        return lambda *_: tuple(jnp.zeros(s.shape, s.dtype) for s in shapes)

    block = pl.pallas_call(
        pack_kernel,
        out_shape=shape_block,
        in_specs=[vmem()] * 2,
        out_specs=vmem(),
        compiler_params=PARAMS,
        name="pack",
    )(a, b)
    chips = [block] + [shift_x(block, k) for k in range(1, X)]

    table = placement_map.reshape(Z * Y, SLOTS)
    pick = jnp.sum(jnp.where(table // TILES == expert, table % TILES, 0), axis=1)
    early_out = choose_tiles(0, EARLY * 128, pick, frozen)
    early = lax.all_to_all(early_out, "expert", split_axis=0, concat_axis=0, tiled=True)
    rest = jax.ShapeDtypeStruct(((n_tiles - EARLY) * LOW_RANK, 128), BF16)
    rows = jax.ShapeDtypeStruct((Z * Y * TILE_ROWS, 128), BF16)

    def gradients(x, g, ids, counts, *chips):
        blocks = [b for mine in chips for b in (mine, swap_core(mine))]
        kept, given = pl.pallas_call(
            gradient_kernel,
            out_shape=[shape_blocks] * 2,
            in_specs=[smem()] * 2 + [vmem()] * (2 + DP),
            out_specs=[vmem()] * 2,
            compiler_params=PARAMS,
            name="gradients",
        )(ids, counts, x, g, *blocks)
        return kept, swap_core(given)

    shape_blocks = jax.ShapeDtypeStruct((X,) + shape_block.shape, BF16)
    kept, taken = lax.cond(
        some, gradients, zeros([shape_blocks] * 2), x, g, ids, counts, *chips
    )
    pairs = pl.pallas_call(
        pair_kernel,
        out_shape=[shape_block] * X,
        in_specs=[vmem()] * 2,
        out_specs=[vmem()] * X,
        compiler_params=PARAMS,
        cost_estimate=HEAVY,
        name="pairs",
    )(kept, taken)
    sums = [pairs[0]] + [shift_x(pairs[k], k) for k in range(1, X)]
    late_base = choose_tiles(EARLY * 128, (n_tiles - EARLY) * 128, pick, frozen)
    sums[-1], late_base = lax.optimization_barrier((sums[-1], late_base))
    b_rows = EARLY * LOW_RANK
    message = jax.ShapeDtypeStruct((Z, b_rows + Y * TILE_ROWS, 128), BF16)
    new_a, new_a1, new_a2, new_b, new_b1, new_b2, messages, b_rest, a_rows = pl.pallas_call(
        adam_kernel,
        out_shape=[shape_a] * 3 + [shape_b] * 3 + [message, rest, rows],
        in_specs=[smem()] * 3 + [vmem()] * (X + 6),
        out_specs=[vmem()] * 9,
        scratch_shapes=[pltpu.VMEM(a.shape, BF16)],
        compiler_params=pltpu.CompilerParams(vmem_limit_bytes=12 * 1024 * 1024),
        name="adam",
    )(ids, pick, counts, *sums, a, a1, a2, b, b1, b2)
    chips = [b_rest] + [shift_x(b_rest, k) for k in range(1, X)]
    messages, early = lax.optimization_barrier((messages, early))
    arrived = lax.all_to_all(
        messages,
        "expert",
        split_axis=0,
        concat_axis=0,
        tiled=True,
        axis_index_groups=[[z * Y + y for z in range(Z)] for y in range(Y)],
    )

    def swap_all(*chips):
        return tuple(b for mine in chips for b in (mine, swap_core(mine)))

    others = lax.cond(some, swap_all, zeros([rest] * DP), *chips)
    mixed = pl.pallas_call(
        mix_kernel,
        out_shape=jax.ShapeDtypeStruct(late_base.shape, BF16),
        in_specs=[smem()] + [vmem()] * (2 + DP),
        out_specs=vmem(),
        compiler_params=pltpu.CompilerParams(vmem_limit_bytes=12 * 1024 * 1024),
        cost_estimate=pl.CostEstimate(flops=4680000000, bytes_accessed=15600000, transcendentals=0),
        name="mix",
    )(ids, late_base, a_rows, *others)
    mixed, arrived = lax.optimization_barrier((mixed, arrived))
    late = lax.all_to_all(mixed, "expert", split_axis=0, concat_axis=0, tiled=True)

    served_early = jax.ShapeDtypeStruct((SLOTS, TILE_ROWS, sizes[0]), BF16)

    def spread(ids, placement_map, early, arrived):
        parts = pl.pallas_call(
            stack_kernel,
            out_shape=[jax.ShapeDtypeStruct((Z, b_rows + TILE_ROWS, 128), BF16)] * Y,
            in_specs=[vmem()],
            out_specs=[vmem()] * Y,
            compiler_params=PARAMS,
            name="stack",
        )(arrived)
        parts = [parts[0]] + [shift_y(parts[dy], dy) for dy in range(1, Y)]
        ups, downs = pl.pallas_call(
            select_kernel,
            out_shape=[
                jax.ShapeDtypeStruct((SLOTS, b_rows, 128), BF16),
                jax.ShapeDtypeStruct((SLOTS, TILE_ROWS, 128), BF16),
            ],
            in_specs=[smem()] * 2 + [vmem()] * Y,
            out_specs=[vmem()] * 2,
            compiler_params=PARAMS,
            name="select",
        )(ids, placement_map, *parts)
        chips = [ups] + [shift_x(ups, k) for k in range(1, X)]
        every = [b for mine in chips for b in (mine, swap_core(mine))]
        return pl.pallas_call(
            early_kernel,
            out_shape=served_early,
            in_specs=[smem()] * 2 + [vmem()] * (2 + DP),
            out_specs=vmem(),
            compiler_params=PARAMS,
            name="early",
        )(ids, placement_map, early, downs, *every)

    def no_spread(*_):
        return jnp.zeros(served_early.shape, BF16)

    first = lax.cond(some, spread, no_spread, ids, placement_map, early, arrived)

    served = pl.pallas_call(
        merge_kernel,
        out_shape=jax.ShapeDtypeStruct((SLOTS, TILE_ROWS, width), BF16),
        in_specs=[smem()] * 2 + [vmem()] * 2,
        out_specs=vmem(),
        compiler_params=pltpu.CompilerParams(vmem_limit_bytes=12 * 1024 * 1024),
        name="merge",
    )(ids, placement_map, first, late)

    return (
        new_a[None],
        new_a1[None],
        new_a2[None],
        new_b[None],
        new_b1[None],
        new_b2[None],
        served[:, None],
    )


def solution(mesh):
    return jax.shard_map(
        per_device,
        mesh=mesh,
        in_specs=(
            P("dp", "expert", None, None),
            P("dp", "expert", None, None),
            P(None, "expert"),
            P("expert", "dp", None),
            P("expert", "dp", None),
            P("expert", "dp", None),
            P("expert", None, "dp"),
            P("expert", None, "dp"),
            P("expert", None, "dp"),
            P("expert", "dp", None),
            P(),
        ),
        out_specs=(
            P("expert", "dp", None),
            P("expert", "dp", None),
            P("expert", "dp", None),
            P("expert", None, "dp"),
            P("expert", None, "dp"),
            P("expert", None, "dp"),
            P("expert", "dp", None, None),
        ),
        check_vma=False,
    )
```

```python
import functools

import jax
import jax.numpy as jnp
from jax import lax
from jax.experimental import pallas as pl
from jax.experimental.pallas import tpu as pltpu
from jax.sharding import PartitionSpec as P

LOW_RANK = 64
TILE_ROWS = 16
TILES = 32
SLOTS = 16
EARLY = 1
LONG = 10**12
Z, Y, DP = 8, 4, 8
X = 4

beta_one = 0.9
beta_two = 0.95
learn_rate = 0.05
adam_eps = 1e-08
bias_one = 1.0 - 0.9**10
bias_two = 1.0 - 0.95**10
adapter_scale = 2.0

F32 = jnp.float32
BF16 = jnp.bfloat16


def adam_step(weights, moment_one, moment_two, gradient):
    moment_one = beta_one * moment_one + (1.0 - beta_one) * gradient
    moment_two = beta_two * moment_two + (1.0 - beta_two) * gradient * gradient
    update_step = (
        learn_rate * (moment_one / bias_one) / (jnp.sqrt(moment_two / bias_two) + adam_eps)
    )
    return (weights - update_step, moment_one, moment_two)


def shift_x(array, k):
    return lax.ppermute(
        array, "dp", [(i, (i // 2 + k) % X * 2 + i % 2) for i in range(DP)]
    )


def swap_core(array):
    return lax.ppermute(array, "dp", [(i, i // 2 * 2 + 1 - i % 2) for i in range(DP)])


def shift_y(array, k):
    return lax.ppermute(
        array, "expert", [(i, i // Y * Y + (i % Y + k) % Y) for i in range(Z * Y)]
    )


def vmem():
    return pl.BlockSpec(memory_space=pltpu.VMEM)


def smem():
    return pl.BlockSpec(memory_space=pltpu.SMEM)


def anywhere():
    return pl.BlockSpec(memory_space=pl.ANY)


PARAMS = pltpu.CompilerParams(vmem_limit_bytes=60 * 1024 * 1024)
HEAVY = pl.CostEstimate(flops=LONG, bytes_accessed=LONG // 100, transcendentals=0)


def gradient_kernel(ids, counts, x, g, *refs):
    blocks, keep, give = refs[:DP], refs[DP], refs[DP + 1]
    chip, core = ids[0] // 2, lax.rem(ids[0], 2)
    live = counts[ids[0]]
    rows = x.shape[0]
    a_rows = x.shape[1] // DP
    cols = g.shape[1] // DP
    tiles = cols // 128
    projected = jnp.zeros((rows, 2 * LOW_RANK), F32)
    gate = jnp.zeros((rows, LOW_RANK), F32)
    up = jnp.zeros((rows, LOW_RANK), F32)
    for i in range(DP):
        k, c = i // 2, i % 2
        j = 2 * lax.rem(chip + X - k, X) + (1 - core if c else core)
        part = x[:, pl.ds(pl.multiple_of(j * a_rows, a_rows), a_rows)]
        projected += jnp.dot(part, blocks[i][:a_rows, :], preferred_element_type=F32)
        b_block = jnp.concatenate(
            [
                blocks[i][a_rows + t * LOW_RANK : a_rows + (t + 1) * LOW_RANK, :]
                for t in range(tiles)
            ],
            axis=1,
        )
        part = g[:, pl.ds(pl.multiple_of(j * cols, 128), cols)]
        term = lax.dot_general(
            part, b_block, (((1,), (1,)), ((), ())), preferred_element_type=F32
        )
        is_gate = j < DP // 2
        gate += jnp.where(is_gate, term, 0.0)
        up += jnp.where(is_gate, 0.0, term)
    mask = lax.broadcasted_iota(jnp.int32, (rows, 2 * LOW_RANK), 0) < live
    backward = jnp.where(mask, jnp.concatenate([gate, up], axis=1), 0.0)
    backward_t = jnp.transpose(backward).astype(BF16)
    projected_t = jnp.transpose(jnp.where(mask, projected, 0.0)).astype(BF16)
    for i in range(DP):
        k, c = i // 2, i % 2
        j = 2 * lax.rem(chip + k, X) + (1 - core if c else core)
        out = give if c else keep
        part = x[:, pl.ds(pl.multiple_of(j * a_rows, a_rows), a_rows)]
        grad = jnp.dot(backward_t, part, preferred_element_type=F32).astype(BF16)
        for t in range(a_rows // 128):
            out[k, t * 128 : (t + 1) * 128, :] = grad[:, t * 128 : (t + 1) * 128]
        part = g[:, pl.ds(pl.multiple_of(j * cols, 128), cols)]
        half = jnp.where(j < DP // 2, projected_t[:LOW_RANK], projected_t[LOW_RANK:])
        grad = jnp.dot(half, part, preferred_element_type=F32).astype(BF16)
        for t in range(tiles):
            out[k, a_rows + t * LOW_RANK : a_rows + (t + 1) * LOW_RANK, :] = grad[
                :, t * 128 : (t + 1) * 128
            ]


def pack_kernel(a, b, out):
    a_rows = a.shape[0]
    out[:a_rows, :] = a[...].astype(BF16)
    for t in range(b.shape[1] // 128):
        r = slice(a_rows + t * LOW_RANK, a_rows + (t + 1) * LOW_RANK)
        out[r, :] = b[:, t * 128 : (t + 1) * 128].astype(BF16)


def pair_kernel(kept, taken, *outs):
    for k in range(X):
        outs[k][...] = (kept[k].astype(F32) + taken[k].astype(F32)).astype(BF16)


def adam_kernel(ids, pick, counts, *refs):
    blocks = refs[:X]
    a, a1, a2, b, b1, b2 = refs[X : X + 6]
    na, na1, na2, nb, nb1, nb2 = refs[X + 6 : X + 12]
    send, rest, rows, ah = refs[X + 12 :]
    tokens = counts[0]
    for p in range(1, DP):
        tokens += counts[p]
    factor = adapter_scale / jnp.full((1, 128), tokens, jnp.int32).astype(F32)
    a_rows = a.shape[0]

    def total(lo, hi):
        s = blocks[0][lo:hi, :].astype(F32)
        for k in range(1, X):
            s += blocks[k][lo:hi, :].astype(F32)
        return s * factor

    for t in range(b.shape[1] // 128):
        c = slice(t * 128, (t + 1) * 128)
        grad = total(a_rows + t * LOW_RANK, a_rows + (t + 1) * LOW_RANK)
        new, one, two = adam_step(b[:, c], b1[:, c], b2[:, c], grad)
        nb[:, c], nb1[:, c], nb2[:, c] = new, one, two
        if t < EARLY:
            for dz in range(Z):
                send[dz, t * LOW_RANK : (t + 1) * LOW_RANK, :] = new.astype(BF16)
        else:
            rest[(t - EARLY) * LOW_RANK : (t - EARLY + 1) * LOW_RANK, :] = new.astype(BF16)
    for t in range(a_rows // 128):
        r = slice(t * 128, (t + 1) * 128)
        grad = jnp.transpose(total(t * 128, (t + 1) * 128))
        new, one, two = adam_step(a[r, :], a1[r, :], a2[r, :], grad)
        na[r, :], na1[r, :], na2[r, :] = new, one, two
        ah[r, :] = new.astype(BF16)
    for owner in range(Z * Y):
        start = pl.multiple_of(pick[owner] * TILE_ROWS, TILE_ROWS)
        rows[owner * TILE_ROWS : (owner + 1) * TILE_ROWS, :] = ah[pl.ds(start, TILE_ROWS), :]
    y = lax.rem(ids[1], Y)
    for dz in range(Z):
        for dy in range(Y):
            owner = dz * Y + lax.rem(y + dy, Y)
            start = pl.multiple_of(owner * TILE_ROWS, TILE_ROWS)
            first = EARLY * LOW_RANK + dy * TILE_ROWS
            send[dz, first : first + TILE_ROWS, :] = rows[pl.ds(start, TILE_ROWS), :]


def tiles_kernel(first, pick, frozen, out):
    cols, part = frozen.shape[1] // DP, out.shape[2] // DP
    for owner in range(Z * Y):
        rows = pl.ds(pl.multiple_of(pick[owner] * TILE_ROWS, TILE_ROWS), TILE_ROWS)
        for j in range(DP):
            start = j * cols + first
            out[owner, :, j * part : (j + 1) * part] = frozen[rows, start : start + part]


def choose_tiles(first, cols, pick, frozen):
    shape = (Z * Y, TILE_ROWS, DP * cols)
    return pl.pallas_call(
        functools.partial(tiles_kernel, first),
        out_shape=jax.ShapeDtypeStruct(shape, BF16),
        in_specs=[smem(), vmem()],
        out_specs=vmem(),
        compiler_params=PARAMS,
        name="tiles",
    )(pick, frozen)


def mix_kernel(ids, late, rows, *refs):
    blocks, out = refs[:DP], refs[DP]
    chip, core = ids[0] // 2, lax.rem(ids[0], 2)
    cols = out.shape[2] // DP
    for i in range(DP):
        k, c = i // 2, i % 2
        j = 2 * lax.rem(chip + X - k, X) + (1 - core if c else core)
        left = jnp.where(j < DP // 2, rows[:, :LOW_RANK], rows[:, LOW_RANK:])
        for t in range(cols // 128):
            right = blocks[i][t * LOW_RANK : (t + 1) * LOW_RANK, :]
            delta = adapter_scale * jnp.dot(left, right, preferred_element_type=F32)
            span = pl.ds(pl.multiple_of(j * cols + t * 128, 128), 128)
            base = late[:, :, span].astype(F32)
            out[:, :, span] = (base + delta.reshape(base.shape)).astype(BF16)


def stack_kernel(arrived, *outs):
    b_rows = arrived.shape[1] - Y * TILE_ROWS
    for dy, out in enumerate(outs):
        first = b_rows + dy * TILE_ROWS
        out[:, :b_rows, :] = arrived[:, :b_rows, :]
        out[:, b_rows:, :] = arrived[:, first : first + TILE_ROWS, :]


def slot_of(ids, table, s):
    source = table[ids[1] * SLOTS + s] // TILES
    dz = source // Y
    dy = lax.rem(lax.rem(ids[1], Y) + Y - lax.rem(source, Y), Y)
    return source, dz, dy


def select_kernel(ids, table, *refs):
    parts, ups, downs = refs[:Y], refs[Y], refs[Y + 1]
    b_rows = ups.shape[1]
    for s in range(SLOTS):
        _, z, dy = slot_of(ids, table, s)
        for i in range(Y):

            @pl.when(dy == i)
            def _(s=s, i=i, z=z):
                ups[s] = parts[i][z, :b_rows, :]
                downs[s] = parts[i][z, b_rows:, :]


def early_kernel(ids, table, early, downs, *refs):
    ups, out = refs[:DP], refs[DP]
    chip, core = ids[0] // 2, lax.rem(ids[0], 2)
    sources = [slot_of(ids, table, s)[0] for s in range(SLOTS)]
    for i in range(DP):
        k, c = i // 2, i % 2
        j = 2 * lax.rem(chip + X - k, X) + (1 - core if c else core)
        is_gate = j < DP // 2
        for s in range(SLOTS):
            left = jnp.where(is_gate, downs[s, :, :LOW_RANK], downs[s, :, LOW_RANK:])
            for t in range(EARLY):
                right = ups[i][s, t * LOW_RANK : (t + 1) * LOW_RANK, :]
                delta = adapter_scale * jnp.dot(left, right, preferred_element_type=F32)
                span = pl.ds(pl.multiple_of((j * EARLY + t) * 128, 128), 128)
                base = early[sources[s], :, span].astype(F32)
                out[s, :, span] = (base + delta).astype(BF16)


def merge_kernel(ids, table, early, late, out):
    one, two = early.shape[2] // DP, late.shape[2] // DP
    for s in range(SLOTS):
        source = slot_of(ids, table, s)[0]
        for j in range(DP):
            start = j * (one + two)
            out[s, :, start : start + one] = early[s, :, j * one : (j + 1) * one]
            start += one
            out[s, :, start : start + two] = late[source, :, j * two : (j + 1) * two]


def per_device(
    x_rows,
    out_grads,
    token_counts,
    a_param,
    a_first,
    a_second,
    b_param,
    b_first,
    b_second,
    frozen_tiles,
    placement_map,
):
    dp, expert = lax.axis_index("dp"), lax.axis_index("expert")
    ids = jnp.stack([dp, expert]).astype(jnp.int32)
    x, g = x_rows[0, 0], out_grads[0, 0]
    a, a1, a2 = a_param[0], a_first[0], a_second[0]
    b, b1, b2 = b_param[0], b_first[0], b_second[0]
    frozen = frozen_tiles[0]
    counts = token_counts.reshape(DP)
    a_rows, width = a.shape[0], frozen.shape[1]
    cols = b.shape[1]
    shape_a, shape_b = jax.ShapeDtypeStruct(a.shape, F32), jax.ShapeDtypeStruct(b.shape, F32)
    shape_block = jax.ShapeDtypeStruct((a_rows + cols // 128 * LOW_RANK, 128), BF16)

    n_tiles = cols // 128
    sizes = [DP * EARLY * 128, DP * (n_tiles - EARLY) * 128]
    halves = [jax.ShapeDtypeStruct((Z * Y, TILE_ROWS, n), BF16) for n in sizes]
    some = dp < DP

    def zeros(shapes):
        return lambda *_: tuple(jnp.zeros(s.shape, s.dtype) for s in shapes)

    block = pl.pallas_call(
        pack_kernel,
        out_shape=shape_block,
        in_specs=[vmem()] * 2,
        out_specs=vmem(),
        compiler_params=PARAMS,
        name="pack",
    )(a, b)
    chips = [block] + [shift_x(block, k) for k in range(1, X)]

    table = placement_map.reshape(Z * Y, SLOTS)
    pick = jnp.sum(jnp.where(table // TILES == expert, table % TILES, 0), axis=1)
    early_out = choose_tiles(0, EARLY * 128, pick, frozen)
    early = lax.all_to_all(early_out, "expert", split_axis=0, concat_axis=0, tiled=True)
    rest = jax.ShapeDtypeStruct(((n_tiles - EARLY) * LOW_RANK, 128), BF16)
    rows = jax.ShapeDtypeStruct((Z * Y * TILE_ROWS, 128), BF16)

    def gradients(x, g, ids, counts, *chips):
        blocks = [b for mine in chips for b in (mine, swap_core(mine))]
        kept, given = pl.pallas_call(
            gradient_kernel,
            out_shape=[shape_blocks] * 2,
            in_specs=[smem()] * 2 + [vmem()] * (2 + DP),
            out_specs=[vmem()] * 2,
            compiler_params=PARAMS,
            name="gradients",
        )(ids, counts, x, g, *blocks)
        return kept, swap_core(given)

    shape_blocks = jax.ShapeDtypeStruct((X,) + shape_block.shape, BF16)
    kept, taken = lax.cond(
        some, gradients, zeros([shape_blocks] * 2), x, g, ids, counts, *chips
    )
    pairs = pl.pallas_call(
        pair_kernel,
        out_shape=[shape_block] * X,
        in_specs=[vmem()] * 2,
        out_specs=[vmem()] * X,
        compiler_params=pltpu.CompilerParams(vmem_limit_bytes=12 * 1024 * 1024),
        cost_estimate=HEAVY,
        name="pairs",
    )(kept, taken)
    sums = [pairs[0]] + [shift_x(pairs[k], k) for k in range(1, X)]
    late_base = choose_tiles(EARLY * 128, (n_tiles - EARLY) * 128, pick, frozen)
    sums[-1], late_base = lax.optimization_barrier((sums[-1], late_base))
    b_rows = EARLY * LOW_RANK
    message = jax.ShapeDtypeStruct((Z, b_rows + Y * TILE_ROWS, 128), BF16)
    new_a, new_a1, new_a2, new_b, new_b1, new_b2, messages, b_rest, a_rows = pl.pallas_call(
        adam_kernel,
        out_shape=[shape_a] * 3 + [shape_b] * 3 + [message, rest, rows],
        in_specs=[smem()] * 3 + [vmem()] * (X + 6),
        out_specs=[vmem()] * 9,
        scratch_shapes=[pltpu.VMEM(a.shape, BF16)],
        compiler_params=pltpu.CompilerParams(vmem_limit_bytes=12 * 1024 * 1024),
        name="adam",
    )(ids, pick, counts, *sums, a, a1, a2, b, b1, b2)
    chips = [b_rest] + [shift_x(b_rest, k) for k in range(1, X)]
    messages, early = lax.optimization_barrier((messages, early))
    arrived = lax.all_to_all(
        messages,
        "expert",
        split_axis=0,
        concat_axis=0,
        tiled=True,
        axis_index_groups=[[z * Y + y for z in range(Z)] for y in range(Y)],
    )

    def swap_all(*chips):
        return tuple(b for mine in chips for b in (mine, swap_core(mine)))

    others = lax.cond(some, swap_all, zeros([rest] * DP), *chips)
    mixed = pl.pallas_call(
        mix_kernel,
        out_shape=jax.ShapeDtypeStruct(late_base.shape, BF16),
        in_specs=[smem()] + [vmem()] * (2 + DP),
        out_specs=vmem(),
        compiler_params=pltpu.CompilerParams(vmem_limit_bytes=12 * 1024 * 1024),
        cost_estimate=pl.CostEstimate(flops=4680000000, bytes_accessed=15600000, transcendentals=0),
        name="mix",
    )(ids, late_base, a_rows, *others)
    mixed, arrived = lax.optimization_barrier((mixed, arrived))
    late = lax.all_to_all(mixed, "expert", split_axis=0, concat_axis=0, tiled=True)

    served_early = jax.ShapeDtypeStruct((SLOTS, TILE_ROWS, sizes[0]), BF16)

    def spread(ids, placement_map, early, arrived):
        parts = pl.pallas_call(
            stack_kernel,
            out_shape=[jax.ShapeDtypeStruct((Z, b_rows + TILE_ROWS, 128), BF16)] * Y,
            in_specs=[vmem()],
            out_specs=[vmem()] * Y,
            compiler_params=pltpu.CompilerParams(vmem_limit_bytes=12 * 1024 * 1024),
            name="stack",
        )(arrived)
        parts = [parts[0]] + [shift_y(parts[dy], dy) for dy in range(1, Y)]
        ups, downs = pl.pallas_call(
            select_kernel,
            out_shape=[
                jax.ShapeDtypeStruct((SLOTS, b_rows, 128), BF16),
                jax.ShapeDtypeStruct((SLOTS, TILE_ROWS, 128), BF16),
            ],
            in_specs=[smem()] * 2 + [vmem()] * Y,
            out_specs=[vmem()] * 2,
            compiler_params=pltpu.CompilerParams(vmem_limit_bytes=12 * 1024 * 1024),
            name="select",
        )(ids, placement_map, *parts)
        chips = [ups] + [shift_x(ups, k) for k in range(1, X)]
        every = [b for mine in chips for b in (mine, swap_core(mine))]
        return pl.pallas_call(
            early_kernel,
            out_shape=served_early,
            in_specs=[smem()] * 2 + [vmem()] * (2 + DP),
            out_specs=vmem(),
            compiler_params=PARAMS,
            name="early",
        )(ids, placement_map, early, downs, *every)

    def no_spread(*_):
        return jnp.zeros(served_early.shape, BF16)

    first = lax.cond(some, spread, no_spread, ids, placement_map, early, arrived)

    served = pl.pallas_call(
        merge_kernel,
        out_shape=jax.ShapeDtypeStruct((SLOTS, TILE_ROWS, width), BF16),
        in_specs=[smem()] * 2 + [vmem()] * 2,
        out_specs=vmem(),
        compiler_params=pltpu.CompilerParams(vmem_limit_bytes=12 * 1024 * 1024),
        name="merge",
    )(ids, placement_map, first, late)

    return (
        new_a[None],
        new_a1[None],
        new_a2[None],
        new_b[None],
        new_b1[None],
        new_b2[None],
        served[:, None],
    )


def solution(mesh):
    return jax.shard_map(
        per_device,
        mesh=mesh,
        in_specs=(
            P("dp", "expert", None, None),
            P("dp", "expert", None, None),
            P(None, "expert"),
            P("expert", "dp", None),
            P("expert", "dp", None),
            P("expert", "dp", None),
            P("expert", None, "dp"),
            P("expert", None, "dp"),
            P("expert", None, "dp"),
            P("expert", "dp", None),
            P(),
        ),
        out_specs=(
            P("expert", "dp", None),
            P("expert", "dp", None),
            P("expert", "dp", None),
            P("expert", None, "dp"),
            P("expert", None, "dp"),
            P("expert", None, "dp"),
            P("expert", "dp", None, None),
        ),
        check_vma=False,
    )
```
